256 devices in a mesh: dp: 32 (over x, y, core), seq: 8 (over z).
Axes of the slice: x: 4, y: 4, z: 8, core: 2. Of those that a mesh axis runs over, the one named last changes fastest.
Arguments:
- tokens: bfloat16 [32, 8, 128, 3072], P('dp', 'seq'), may hold values from -6 to 6
- d_attn: bfloat16 [32, 8, 128, 2048], P('dp', 'seq'), may hold values from -0.75 to 0.75
- frame_counts: int32 [32], P('dp'), may hold values from 2 to 8, as said below
- w_query: bfloat16 [3072, 2048], P('dp', 'seq'), may hold values from -0.109375 to 0.109375
- w_key: bfloat16 [3072, 2048], P('dp', 'seq'), may hold values from -0.109375 to 0.109375
- w_value: bfloat16 [3072, 2048], P('dp', 'seq'), may hold values from -0.109375 to 0.109375
Outputs:
- attn: bfloat16 [32, 8, 128, 2048], P('dp', 'seq')
- d_tokens: bfloat16 [32, 8, 128, 3072], P('dp', 'seq')
- grad_query: float32 [3072, 2048], P('dp', 'seq')
- grad_key: float32 [3072, 2048], P('dp', 'seq')
- grad_value: float32 [3072, 2048], P('dp', 'seq')
The draws below stay inside these ranges and needn't reach their ends.
Inputs may be any that keep to these rules, and one draw needn't show every extreme that they name: `frame_counts`: some clip has all 8 frames in every draw; every clip has at least two.
All inputs are finite; a program needn't handle non-finite values.
Results may differ from the reference program's by a relative error of at most 0.018.
Values may be sent and summed in bfloat16 or wider, within the bound.
A program may use at most 128 MiB of HBM per device.

```python
import jax
import jax.numpy as jnp
from jax import lax

D = 3072
HEAD_DIM = 128
S = 128
HD = 2048
FRAMES = 8
N_DP = 32
N_SEQ = 8


def draw_tokens(key, part):
    key = jax.random.fold_in(key, 11)
    shape = (N_DP, FRAMES, S, D)
    values = jnp.clip(jax.random.normal(key, shape, jnp.float32), -6.0, 6.0)
    return values.astype(jnp.bfloat16)


def draw_frame_counts(key, part):
    key = jax.random.fold_in(key, 23)
    first, second = jax.random.split(key)
    counts = jax.random.randint(first, (N_DP,), 2, FRAMES + 1)
    full_clip = jax.random.randint(second, (), 0, N_DP)
    return jnp.where(jnp.arange(N_DP) == full_clip, FRAMES, counts).astype(jnp.int32)


def steps_of(rng, extent, cuts, low, top_value):
    level, own = 1.0, jax.random.fold_in(rng, 6)
    for dim, parts in cuts:
        draws = jnp.exp(jax.random.uniform(jax.random.fold_in(own, dim), (parts,), jnp.float32, low / len(cuts), top_value / len(cuts)))
        level = level * jnp.repeat(draws, extent[dim] // parts).reshape([-1 if axis == dim else 1 for axis in range(len(extent))])
    return level


def noise(own_key, extent, scale, bound, cuts=(), held_as=jnp.bfloat16):
    array = scale * jax.random.normal(own_key, extent, jnp.float32)
    if cuts:
        array = array * steps_of(own_key, extent, cuts, -0.22, 0.18)
    return jnp.clip(array, -bound, bound).astype(held_as)


def setup_inputs(seed: int = 0) -> dict:
    streams_of = jax.random.split(jax.random.key(seed), 7)
    tokens = draw_tokens(jax.random.fold_in(streams_of[6], 71), 0)
    d_attn = noise(streams_of[1], (N_DP, FRAMES, S, HD), 0.125, 0.75, ((0, 32), (1, 8)))
    frame_counts = draw_frame_counts(jax.random.fold_in(streams_of[6], 71), 0)
    w_query = noise(streams_of[3], (D, HD), D ** -0.5, 0.109375, ((0, 32), (1, 8)))
    w_key = noise(streams_of[4], (D, HD), D ** -0.5, 0.109375, ((0, 32), (1, 8)))
    w_value = noise(streams_of[5], (D, HD), D ** -0.5, 0.109375, ((0, 32), (1, 8)))
    return {"tokens": tokens, "d_attn": d_attn, "frame_counts": frame_counts, "w_query": w_query, "w_key": w_key, "w_value": w_value}


def rotary_tables(frames):
    half = HEAD_DIM // 2
    inv = 10000.0 ** (-(2.0 * jnp.arange(half, dtype=jnp.float32)) / HEAD_DIM)
    angle = jnp.arange(frames, dtype=jnp.float32)[:, None] * inv[None, :]
    return jnp.cos(angle)[:, None, None, :], jnp.sin(angle)[:, None, None, :]


def rotate(vec, cosine, sine):
    half = HEAD_DIM // 2
    first, second = vec[..., :half], vec[..., half:]
    return jnp.concatenate([first * cosine - second * sine, first * sine + second * cosine], axis=-1)


def unrotate(grad, cosine, sine):
    half = HEAD_DIM // 2
    first, second = grad[..., :half], grad[..., half:]
    return jnp.concatenate([first * cosine + second * sine, second * cosine - first * sine], axis=-1)


def attend(query, keys, values, count, frames):
    scale = HEAD_DIM ** -0.5
    scores = jnp.einsum('fshe,gshe->hfgs', query.astype(jnp.float32), keys.astype(jnp.float32), precision=lax.Precision.HIGHEST) * scale
    key_live = jnp.arange(frames) < count
    scores = jnp.where(key_live[None, None, :, None], scores, jnp.float32(-1e30))
    top = jnp.max(scores, axis=2, keepdims=True)
    expo = jnp.exp(scores - top)
    probs = expo / jnp.sum(expo, axis=2, keepdims=True)
    probs_b = probs.astype(jnp.bfloat16)
    output = jnp.einsum('hfgs,gshe->fshe', probs_b.astype(jnp.float32), values.astype(jnp.float32), precision=lax.Precision.HIGHEST)
    return output.astype(jnp.bfloat16), probs, probs_b


def attend_back(grad_out, query, keys, values, probs, probs_b, cosine, sine):
    scale = HEAD_DIM ** -0.5
    grad_f = grad_out.astype(jnp.float32)
    d_values = jnp.einsum('hfgs,fshe->gshe', probs_b.astype(jnp.float32), grad_f, precision=lax.Precision.HIGHEST).astype(jnp.bfloat16)
    d_probs = jnp.einsum('fshe,gshe->hfgs', grad_f, values.astype(jnp.float32), precision=lax.Precision.HIGHEST)
    inner = jnp.sum(probs * d_probs, axis=2, keepdims=True)
    d_scores = probs * (d_probs - inner) * scale
    dq_rot = jnp.einsum('hfgs,gshe->fshe', d_scores, keys.astype(jnp.float32), precision=lax.Precision.HIGHEST)
    dk_rot = jnp.einsum('hfgs,fshe->gshe', d_scores, query.astype(jnp.float32), precision=lax.Precision.HIGHEST)
    d_query = unrotate(dq_rot, cosine, sine).astype(jnp.bfloat16)
    d_keys = unrotate(dk_rot, cosine, sine).astype(jnp.bfloat16)
    return d_query, d_keys, d_values


def reference(tokens, d_attn, frame_counts, w_query, w_key, w_value):
    frames = tokens.shape[1]
    spatial = tokens.shape[2]
    width = tokens.shape[3]
    total = w_query.shape[1]
    local = total // N_SEQ
    cosine, sine = rotary_tables(frames)

    def one_clip(carry, items):
        clip, grad_out, count = items
        flat = clip.reshape(frames * spatial, width)
        shape = (frames, spatial, total // HEAD_DIM, HEAD_DIM)
        pre_q = jnp.dot(flat, w_query, preferred_element_type=jnp.float32).reshape(shape)
        pre_k = jnp.dot(flat, w_key, preferred_element_type=jnp.float32).reshape(shape)
        pre_v = jnp.dot(flat, w_value, preferred_element_type=jnp.float32).reshape(shape)
        query = rotate(pre_q, cosine, sine).astype(jnp.bfloat16)
        keys = rotate(pre_k, cosine, sine).astype(jnp.bfloat16)
        values = pre_v.astype(jnp.bfloat16)
        output, probs, probs_b = attend(query, keys, values, count, frames)
        d_query, d_keys, d_values = attend_back(grad_out.reshape(shape), query, keys, values, probs, probs_b, cosine, sine)
        dq_flat = d_query.reshape(frames * spatial, total)
        dk_flat = d_keys.reshape(frames * spatial, total)
        dv_flat = d_values.reshape(frames * spatial, total)
        terms = (jnp.dot(flat.T, dq_flat, preferred_element_type=jnp.float32),
                 jnp.dot(flat.T, dk_flat, preferred_element_type=jnp.float32),
                 jnp.dot(flat.T, dv_flat, preferred_element_type=jnp.float32))
        summed = jnp.zeros((frames * spatial, width), jnp.float32)
        for group in range(N_SEQ):
            low = group * local
            part = jnp.dot(dq_flat[:, low:low + local], w_query[:, low:low + local].T, preferred_element_type=jnp.float32)
            part = part + jnp.dot(dk_flat[:, low:low + local], w_key[:, low:low + local].T, preferred_element_type=jnp.float32)
            part = part + jnp.dot(dv_flat[:, low:low + local], w_value[:, low:low + local].T, preferred_element_type=jnp.float32)
            summed = summed + part.astype(jnp.bfloat16).astype(jnp.float32)
        carry = (carry[0] + terms[0], carry[1] + terms[1], carry[2] + terms[2])
        return carry, (output.reshape(frames, spatial, total), summed.astype(jnp.bfloat16).reshape(frames, spatial, width))

    zeros = jnp.zeros((width, total), jnp.float32)
    grads, outs = lax.scan(one_clip, (zeros, zeros, zeros), (tokens, d_attn, frame_counts))
    return outs[0], outs[1], grads[0], grads[1], grads[2]
```

```python
import functools

import jax
import jax.numpy as jnp
import numpy as np
from jax import lax
from jax.experimental import pallas as pl
from jax.experimental.pallas import tpu as pltpu
from jax.sharding import PartitionSpec as P

HEAD_DIM = 128
F = 8
S = 128
D = 3072
C = 256
HALF = D // 2
PARTS = 2
SP = S // PARTS
MESH = pl.DeviceIdType.MESH
BF = jnp.bfloat16
F32 = jnp.float32


def dot_nt(a, b):
    return lax.dot_general(a, b, (((1,), (1,)), ((), ())), preferred_element_type=F32)


def dot_tn(a, b):
    return lax.dot_general(a, b, (((0,), (0,)), ((), ())), preferred_element_type=F32)


def dot_nn(a, b):
    return jnp.dot(a, b, preferred_element_type=F32)


def kernel(
    cnt_ref, tok_ref, da_ref, wq_ref, wk_ref, wv_ref, cos_ref, sin_ref,
    attn_ref, dtok_ref, gq_ref, gk_ref, gv_ref,
    X, W, GA, QKV, DD, O, Y, RS, G, SIBS, SIBR, PAIR, GR,
    loc_sem, ag_s, ag_r, wd_s, wd_r, wf_s, wf_r, da_s, da_r, at_s, at_r,
    rs_s, rs_r, sb_s, sb_r, gd_s, gd_r,
):
    dp = lax.axis_index("dp")
    me = lax.axis_index("seq")
    core = lax.rem(dp, 2)
    chip = dp // 2
    cx = chip // 4
    cy = lax.rem(chip, 4)
    sib = dp + 1 - 2 * core

    def fr(i):
        return lax.rem(me + (i + 16), 8)

    def chip_at(o):
        return lax.rem(cx + o // 4, 4) * 4 + lax.rem(cy + o % 4, 4)

    def chip_from(o):
        return lax.rem(cx + 4 - o // 4, 4) * 4 + lax.rem(cy + 4 - o % 4, 4)

    def remote(src, dst, ssem, rsem, dev):
        return pltpu.make_async_remote_copy(
            src_ref=src, dst_ref=dst, send_sem=ssem, recv_sem=rsem,
            device_id=dev, device_id_type=MESH,
        )

    loc = [
        pltpu.make_async_copy(tok_ref, X.at[me], loc_sem.at[0]),
        pltpu.make_async_copy(wq_ref, W.at[dp, :, 0:C], loc_sem.at[1]),
        pltpu.make_async_copy(wk_ref, W.at[dp, :, C:2 * C], loc_sem.at[2]),
        pltpu.make_async_copy(wv_ref, W.at[dp, :, 2 * C:3 * C], loc_sem.at[3]),
    ]
    for c in loc:
        c.start()

    bar = pltpu.get_barrier_semaphore()
    for i in range(1, 8):
        pl.semaphore_signal(bar, inc=1, device_id=(dp, fr(i)), device_id_type=MESH)
    for o in range(1, 16):
        pl.semaphore_signal(bar, inc=1, device_id=(chip_at(o) * 2 + core, me), device_id_type=MESH)
    pl.semaphore_signal(bar, inc=1, device_id=(sib, me), device_id_type=MESH)
    pl.semaphore_wait(bar, 23)
    for c in loc:
        c.wait()

    nbr = ((dp, fr(1)), (dp, fr(-1)))

    def cols(sub):
        return slice(0, HALF) if sub == 0 else slice(HALF, D)

    def sub_of(d, k):
        return (k % 2) if d == 0 else 1 - (k % 2)

    def ag_copy(p, d, k):
        hop = k // 2
        f = fr(-hop) if d == 0 else fr(hop)
        ref = X.at[f, slice(p * SP, (p + 1) * SP), cols(sub_of(d, k))]
        return remote(ref, ref, ag_s.at[p, d, k], ag_r.at[p, d, k], nbr[d])

    def ag_wait(p, d, k):
        hop = k // 2
        f = fr(-1 - hop) if d == 0 else fr(1 + hop)
        ref = X.at[f, slice(p * SP, (p + 1) * SP), cols(sub_of(d, k))]
        remote(ref, ref, ag_s.at[p, d, k], ag_r.at[p, d, k], nbr[d]).wait_recv()

    def ag_begin(p):
        for k in (0, 1):
            for d in (0, 1):
                ag_copy(p, d, k).start()

    def ag_pump(p, k):
        for d in (0, 1):
            ag_wait(p, d, k)
            if k + 2 <= 6:
                ag_copy(p, d, k + 2).start()

    def wd_copy(o):
        return remote(W.at[dp], W.at[dp], wd_s.at[o], wd_r.at[o], (chip_at(o) * 2 + core, me))

    def wf_copy(o):
        blk = chip_from(o) * 2 + core
        return remote(W.at[blk], W.at[blk], wf_s.at[o], wf_r.at[o], (sib, me))

    def w_service(o):
        blk = chip_from(o) * 2 + core
        remote(W.at[blk], W.at[blk], wd_s.at[o], wd_r.at[o], (sib, me)).wait_recv()
        wf_copy(o).start()

    order = [1, 3, 4, 12, 5, 7, 13, 15, 2, 8, 6, 14, 9, 11, 10]

    ag_begin(0)
    wf_copy(0).start()
    for o in order:
        wd_copy(o).start()

    def da_copy(i):
        j = fr(i)
        return remote(
            da_ref.at[:, pl.ds(pl.multiple_of(j * C, C), C)], GA.at[me],
            da_s.at[i], da_r.at[i], (dp, j),
        )

    w_i = 0
    for k in range(7):
        ag_pump(0, k)
        if k == 4:
            ag_begin(1)
            for i in (1, 7, 2, 6, 3, 5, 4):
                da_copy(i).start()
        take = 2 if k < 6 else 3
        for o in order[w_i:w_i + take]:
            w_service(o)
        w_i += take
    own_g = pltpu.make_async_copy(
        da_ref.at[:, pl.ds(pl.multiple_of(me * C, C), C)], GA.at[me], loc_sem.at[4])
    own_g.start()

    for o in range(16):
        blk = chip_from(o) * 2 + 1 - core
        remote(W.at[blk], W.at[blk], wf_s.at[o], wf_r.at[o], (sib, me)).wait_recv()

    row = lax.broadcasted_iota(jnp.int32, (128, 128), 0)
    col = lax.broadcasted_iota(jnp.int32, (128, 128), 1)
    live = (jnp.bitwise_and(row, 15) == jnp.bitwise_and(col, 15)) & (
        lax.shift_right_logical(col, 4) < cnt_ref[0])
    scale = HEAD_DIM ** -0.5
    bias = jnp.where(live, jnp.float32(0.0), jnp.float32(-1e30))

    def proj(p, grp):
        rows = slice(p * SP, (p + 1) * SP)
        x = X[4 * grp:4 * grp + 4, rows, :].reshape(4 * SP, D)
        cosv = cos_ref[4 * grp:4 * grp + 4, :].reshape(4, 1, 128)
        sinv = sin_ref[4 * grp:4 * grp + 4, :].reshape(4, 1, 128)
        for c in range(3):
            w = W[:, :, c * C:(c + 1) * C].reshape(D, C)
            pre = dot_nn(x, w)
            for h in range(2):
                u = pre[:, h * 128:(h + 1) * 128]
                if c < 2:
                    r = pltpu.roll(u, 64, 1).reshape(4, SP, 128)
                    u = u.reshape(4, SP, 128) * cosv + r * sinv
                QKV[c, 4 * grp:4 * grp + 4, :, h * 128:(h + 1) * 128] = (
                    u.reshape(4, SP, 128).astype(BF))

    def attend(p, b, h):
        sl = slice(b * 16, (b + 1) * 16)
        gsl = slice(p * SP + b * 16, p * SP + (b + 1) * 16)
        hc = slice(h * 128, (h + 1) * 128)
        q = QKV[0, :, sl, hc].reshape(128, 128)
        k = QKV[1, :, sl, hc].reshape(128, 128)
        v = QKV[2, :, sl, hc].reshape(128, 128)
        g = GA[:, gsl, hc].reshape(128, 128)
        s = dot_nt(q, k) * scale + bias
        top = jnp.max(s, axis=1, keepdims=True)
        e = jnp.exp(s - top)
        prob = e / jnp.sum(e, axis=1, keepdims=True)
        pb = prob.astype(BF)
        O[p, :, sl, hc] = dot_nn(pb, v).astype(BF).reshape(8, 16, 128)
        dv = dot_tn(pb, g)
        dpr = dot_nt(g, v)
        inner = jnp.sum(prob * dpr, axis=1, keepdims=True)
        ds = prob * (dpr - inner) * scale
        hi = ds.astype(BF)
        lo = (ds - hi.astype(F32)).astype(BF)
        dq = dot_nn(hi, k) + dot_nn(lo, k)
        dk = dot_tn(hi, q) + dot_tn(lo, q)
        cosv = cos_ref[...].reshape(8, 1, 128)
        sinv = sin_ref[...].reshape(8, 1, 128)
        for c, t in ((0, dq), (1, dk)):
            r = pltpu.roll(t, 64, 1).reshape(8, 16, 128)
            un = t.reshape(8, 16, 128) * cosv - r * sinv
            DD[:, sl, c * C + h * 128:c * C + (h + 1) * 128] = un.astype(BF)
        DD[:, sl, 2 * C + h * 128:2 * C + (h + 1) * 128] = dv.astype(BF).reshape(8, 16, 128)

    def at_copy(p, i):
        f = fr(i)
        rows = slice(p * SP, (p + 1) * SP)
        return remote(
            O.at[p, f], attn_ref.at[rows, pl.ds(pl.multiple_of(me * C, C), C)],
            at_s.at[p, i], at_r.at[p, i], (dp, f),
        )

    def at_own(p):
        rows = slice(p * SP, (p + 1) * SP)
        return pltpu.make_async_copy(
            O.at[p, me], attn_ref.at[rows, pl.ds(pl.multiple_of(me * C, C), C)],
            loc_sem.at[5 + p])

    def at_begin(p):
        at_own(p).start()
        for i in (1, 7, 2, 6, 3, 5, 4):
            at_copy(p, i).start()

    def grads(p):
        rows = slice(p * SP, (p + 1) * SP)

        def body(i, _):
            x = X[:, rows, pl.ds(pl.multiple_of(i * 384, 384), 384)].reshape(F * SP, 384)
            t = dot_tn(x, DD[...].reshape(F * SP, 3 * C)).reshape(4, 96, 3 * C)
            if p == 0:
                G[pl.ds(4 * i, 4)] = t
            else:
                G[pl.ds(4 * i, 4)] += t
            return 0

        lax.fori_loop(0, 8, body, 0)

    def partial(p):
        def body(i, _):
            w = W[pl.ds(i * 8, 8)].reshape(768, 3 * C)
            t = dot_nt(DD[...].reshape(F * SP, 3 * C), w)
            Y[p, :, :, pl.ds(pl.multiple_of(i * 768, 768), 768)] = (
                t.astype(BF).reshape(F, SP, 768))
            return 0

        lax.fori_loop(0, 4, body, 0)

    def rs_off(k):
        return 4 - k // 2 if k % 2 == 0 else 3 - k // 2

    def rs_copy(p, d, k):
        off = rs_off(k)
        o = fr(off) if d == 0 else fr(-off)
        return remote(
            Y.at[p, o, :, cols(sub_of(d, k))], RS.at[p, d, k],
            rs_s.at[p, d, k], rs_r.at[p, d, k], nbr[d])

    def rs_begin(p):
        for k in (0, 1):
            for d in (0, 1):
                rs_copy(p, d, k).start()

    def rs_pump(p, k):
        for d in (0, 1):
            slot = RS.at[p, d, k]
            remote(slot, slot, rs_s.at[p, d, k], rs_r.at[p, d, k], nbr[d]).wait_recv()
            off = rs_off(k) - 1
            if off >= 1:
                o = fr(off) if d == 0 else fr(-off)
                cs = cols(sub_of(d, k))
                Y[p, o, :, cs] = (Y[p, o, :, cs].astype(F32) + RS[p, d, k].astype(F32)).astype(BF)
                rs_copy(p, d, k + 2).start()

    def rs_final(p):
        rows = slice(p * SP, (p + 1) * SP)
        for sub in (0, 1):
            ka, kb = (6, 5) if sub == 0 else (5, 6)
            dtok_ref[rows, cols(sub)] = (
                Y[p, me, :, cols(sub)].astype(F32)
                + RS[p, 0, ka].astype(F32) + RS[p, 1, kb].astype(F32)).astype(BF)

    proj(0, 0)
    ag_pump(1, 0)
    proj(0, 1)
    ag_pump(1, 1)
    own_g.wait()
    for i in range(1, 8):
        slot = GA.at[fr(i)]
        remote(slot, slot, da_s.at[8 - i], da_r.at[8 - i], nbr[0]).wait_recv()
    for b in range(SP // 16):
        for h in range(2):
            attend(0, b, h)
        if b < 2:
            ag_pump(1, 2 + b)
    at_begin(0)
    partial(0)
    ag_pump(1, 4)
    rs_begin(0)
    grads(0)
    ag_pump(1, 5)
    ag_pump(1, 6)

    proj(1, 0)
    rs_pump(0, 0)
    proj(1, 1)
    rs_pump(0, 1)
    for b in range(SP // 16):
        for h in range(2):
            attend(1, b, h)
        if b < 2:
            rs_pump(0, 2 + b)
    at_begin(1)
    grads(1)
    rs_pump(0, 4)

    def sib_copy(i):
        return remote(SIBS.at[i], SIBR.at[i], sb_s.at[i], sb_r.at[i], (sib, me))

    def sib_send(i, _):
        SIBS[i] = G[2 * i + 1 - core].astype(BF)
        sib_copy(i).start()
        return 0

    lax.fori_loop(0, 16, sib_send, 0)
    partial(1)
    rs_begin(1)
    rs_pump(0, 5)
    rs_pump(0, 6)
    rs_final(0)

    def gd_copy(o):
        i = chip_at(o)
        return remote(PAIR.at[o], GR.at[o], gd_s.at[o], gd_r.at[o], (i * 2 + core, me))

    def sib_wait(i, _):
        sib_copy(i).wait_recv()
        return 0

    lax.fori_loop(0, 16, sib_wait, 0)

    def pair_send(o, _):
        i = chip_at(o)
        PAIR[o] = (G[2 * i + core] + SIBR[i].astype(F32)).astype(BF)
        gd_copy(o).start()
        return 0

    lax.fori_loop(1, 16, pair_send, 0)
    for k in range(7):
        rs_pump(1, k)
    rs_final(1)

    def gd_wait(o, _):
        gd_copy(o).wait_recv()
        return 0

    lax.fori_loop(1, 16, gd_wait, 0)
    total = G[2 * chip + core] + SIBR[chip].astype(F32)
    total = lax.fori_loop(1, 16, lambda o, acc: acc + GR[o].astype(F32), total)
    gq_ref[...] = total[:, 0:C]
    gk_ref[...] = total[:, C:2 * C]
    gv_ref[...] = total[:, 2 * C:3 * C]

    for p in range(PARTS):
        at_own(p).wait()
        for i in range(1, 8):
            rows = slice(p * SP, (p + 1) * SP)
            f = fr(-i)
            slot = attn_ref.at[rows, pl.ds(pl.multiple_of(f * C, C), C)]
            remote(slot, slot, at_s.at[p, i], at_r.at[p, i], nbr[0]).wait_recv()
    for p in range(PARTS):
        for d in (0, 1):
            for k in range(7):
                ag_copy(p, d, k).wait_send()
                rs_copy(p, d, k).wait_send()
        for i in range(1, 8):
            at_copy(p, i).wait_send()
    for i in range(1, 8):
        da_copy(i).wait_send()
    for o in range(1, 16):
        wd_copy(o).wait_send()
        gd_copy(o).wait_send()
    for o in range(16):
        wf_copy(o).wait_send()
        sib_copy(o).wait_send()


def tables():
    half = HEAD_DIM // 2
    inv = 10000.0 ** (-(2.0 * np.arange(half, dtype=np.float32)) / HEAD_DIM)
    angle = np.arange(F, dtype=np.float32)[:, None] * inv[None, :].astype(np.float32)
    c, s = np.cos(angle), np.sin(angle)
    return (np.concatenate([c, c], 1).astype(np.float32),
            np.concatenate([-s, s], 1).astype(np.float32))


def on_device(tokens, d_attn, frame_counts, w_query, w_key, w_value):
    cosine, sine = tables()
    any_ = pl.BlockSpec(memory_space=pl.ANY)
    vmem = pl.BlockSpec(memory_space=pltpu.VMEM)
    smem = pl.BlockSpec(memory_space=pltpu.SMEM)
    dma = pltpu.SemaphoreType.DMA
    blk = (96, 3 * C)
    outs = pl.pallas_call(
        kernel,
        out_shape=(
            jax.ShapeDtypeStruct((S, F * C), BF),
            jax.ShapeDtypeStruct((S, D), BF),
            jax.ShapeDtypeStruct((96, C), F32),
            jax.ShapeDtypeStruct((96, C), F32),
            jax.ShapeDtypeStruct((96, C), F32),
        ),
        in_specs=[smem, any_, vmem, any_, any_, any_, vmem, vmem],
        out_specs=(vmem,) * 5,
        scratch_shapes=[
            pltpu.VMEM((F, S, D), BF),
            pltpu.VMEM((32,) + blk, BF),
            pltpu.VMEM((F, S, C), BF),
            pltpu.VMEM((3, F, SP, C), BF),
            pltpu.VMEM((F, SP, 3 * C), BF),
            pltpu.VMEM((PARTS, F, SP, C), BF),
            pltpu.VMEM((PARTS, F, SP, D), BF),
            pltpu.VMEM((PARTS, 2, 7, SP, HALF), BF),
            pltpu.VMEM((32,) + blk, F32),
            pltpu.VMEM((16,) + blk, BF),
            pltpu.VMEM((16,) + blk, BF),
            pltpu.VMEM((16,) + blk, BF),
            pltpu.VMEM((16,) + blk, BF),
            dma((8,)),
            dma((PARTS, 2, 7)), dma((PARTS, 2, 7)),
            dma((16,)), dma((16,)),
            dma((16,)), dma((16,)),
            dma((8,)), dma((8,)),
            dma((PARTS, 8)), dma((PARTS, 8)),
            dma((PARTS, 2, 7)), dma((PARTS, 2, 7)),
            dma((16,)), dma((16,)),
            dma((16,)), dma((16,)),
        ],
        compiler_params=pltpu.CompilerParams(
            collective_id=0, has_side_effects=True, vmem_limit_bytes=62 * 1024 * 1024),
        name="temporal_attention",
    )(
        frame_counts, tokens.reshape(S, D), d_attn.reshape(S, F * C),
        w_query, w_key, w_value, jnp.asarray(cosine), jnp.asarray(sine),
    )
    attn, dtok, gq, gk, gv = outs
    return attn.reshape(d_attn.shape), dtok.reshape(tokens.shape), gq, gk, gv


def solution(mesh):
    return jax.shard_map(
        on_device,
        mesh=mesh,
        in_specs=(
            P("dp", "seq", None, None),
            P("dp", "seq", None, None),
            P("dp"),
            P("dp", "seq"),
            P("dp", "seq"),
            P("dp", "seq"),
        ),
        out_specs=(
            P("dp", "seq", None, None),
            P("dp", "seq", None, None),
            P("dp", "seq"),
            P("dp", "seq"),
            P("dp", "seq"),
        ),
        check_vma=False,
    )
```

```python
import functools

import jax
import jax.numpy as jnp
import numpy as np
from jax import lax
from jax.experimental import pallas as pl
from jax.experimental.pallas import tpu as pltpu
from jax.sharding import PartitionSpec as P

HEAD_DIM = 128
F = 8
S = 128
D = 3072
C = 256
Q = 32
T = 3 * HEAD_DIM
MESH = pl.DeviceIdType.MESH
BF = jnp.bfloat16
F32 = jnp.float32
ZOFF = (1, -1, 3, -3)


def dot_nt(a, b):
    return lax.dot_general(a, b, (((1,), (1,)), ((), ())), preferred_element_type=F32)


def dot_tn(a, b):
    return lax.dot_general(a, b, (((0,), (0,)), ((), ())), preferred_element_type=F32)


def dot_nn(a, b):
    return jnp.dot(a, b, preferred_element_type=F32)


def kernel(
    cnt_ref, tok_ref, da_ref, wq_ref, wk_ref, wv_ref, cos_ref, sin_ref,
    attn_ref, dtok_ref, gq_ref, gk_ref, gv_ref,
    X, XT, PK, W, GA, QKV, DD, O, Y, GS, HR, R1, LR, R2, ZR, SYS, SYR, PS, PR, TD, CB,
    loc_sem, zw_s, zw_r, ag_s, ag_r, tx_s, tx_r, tp_s, tp_r, ts_s, ts_r, da_s, da_r,
    at_s, at_r, rs_s, rs_r, zr_s, zr_r, sy_s, sy_r, pp_s, pp_r, td_s, td_r, cb_s, cb_r, lt_s, lt_r, rl_s, rl_r,
):
    dp = lax.axis_index("dp")
    me = lax.axis_index("seq")
    core = lax.rem(dp, 2)
    chip = dp // 2
    cx = chip // 4
    cy = lax.rem(chip, 4)
    par = lax.rem(me, 2)
    sg = 2 * par - 1
    quarter = me // 2

    def zz(i):
        return lax.rem(me + (i + 16), 8)

    def m4(i):
        return lax.rem(i + 8, 4)

    def at(k, z):
        return (chip * 2 + k, z)

    def other(dc):
        return core if dc == 0 else 1 - core

    def rows_of(z):
        return pl.ds(pl.multiple_of((z // 2) * Q, Q), Q)

    def group_of(k, z, g):
        return (1 - lax.rem(z, 2)) + 2 * k + 4 * g

    def cols_of(k, z, g):
        return pl.ds(pl.multiple_of(group_of(k, z, g) * C, C), C)

    sib = at(1 - core, me)
    partner = at(core, zz(-sg))

    def remote(src, dst, ssem, rsem, dev):
        return pltpu.make_async_remote_copy(
            src_ref=src, dst_ref=dst, send_sem=ssem, recv_sem=rsem,
            device_id=dev, device_id_type=MESH,
        )

    def arrived(ref, ssem, rsem):
        remote(ref, ref, ssem, rsem, sib).wait_recv()

    loc = []
    for t, w in enumerate((wq_ref, wk_ref, wv_ref)):
        for u in (0, 1):
            loc.append(pltpu.make_async_copy(
                w.at[:, u * 128:(u + 1) * 128], PK.at[u, :, t * 128:(t + 1) * 128],
                loc_sem.at[2 * t + u]))
    own_x = pltpu.make_async_copy(tok_ref.at[rows_of(me)], X.at[core, me], loc_sem.at[6])
    for c in loc:
        c.start()
    own_x.start()

    bar = pltpu.get_barrier_semaphore()

    def greet(dev):
        pl.semaphore_signal(bar, inc=1, device_id=dev, device_id_type=MESH)

    def ring(axis, i):
        if axis == 0:
            return (m4(cx + i) * 8 + cy * 2 + core, me)
        return (cx * 8 + m4(cy + i) * 2 + core, me)

    for i in range(1, 8):
        greet(at(core, zz(i)))
        greet(at(1 - core, zz(i)))
    greet(sib)
    for axis in (0, 1):
        greet(ring(axis, 1))
        greet(ring(axis, -1))
        greet(ring(axis, 2))
    pl.semaphore_wait(bar, 21)

    def zw_copy(t, u):
        return remote(
            PK.at[u], W.at[me // 4, u, cx, cy, core], zw_s.at[t, u],
            zw_r.at[me // 4, u, core], at(lax.rem(me // 2, 2), zz(ZOFF[t])))

    def zw_wait(g, u):
        for k in (0, 1):
            arrived(W.at[g, u, cx, cy, k], zw_s.at[0, u], zw_r.at[g, u, k])

    def axis_of(v, ph):
        return v if ph == 0 else 1 - v

    def pos_of(axis):
        return cx if axis == 0 else cy

    def heavy(ref, v, p, h):
        return ref.at[2 * h:2 * h + 2, p, v] if v == 0 else ref.at[p, 2 * h:2 * h + 2, v]

    def light(ref, v, p):
        return ref.at[p, cy, v] if v == 0 else ref.at[cx, p, v]

    def lt_copy(st, v, i, recv=False):
        g, u = st
        axis = axis_of(v, 0)
        ref = light(W.at[g, u], v, m4(pos_of(axis) - (i if recv else 0)))
        j = g * 4 + u * 2 + v
        return remote(ref, ref, lt_s.at[j, i], lt_r.at[j, i], ring(axis, i))

    def lt_start(st):
        for i in (1, 3, 2):
            for v in (0, 1):
                lt_copy(st, v, i).start()

    def lt_done(st):
        for i in (1, 3, 2):
            for v in (0, 1):
                lt_copy(st, v, i, True).wait_recv()

    def ag_copy(st, v, d, n, recv=False):
        g, u = st
        step = 1 if d == 0 else -1
        axis = axis_of(v, 1)
        back = (1 if n == 2 else 0) + (1 if recv else 0)
        p = m4(pos_of(axis) - step * back)
        h = d if n != 1 else 1 - d
        ref = heavy(W.at[g, u], v, p, h)
        i = g * 4 + u * 2 + v
        return remote(ref, ref, ag_s.at[i, d, n], ag_r.at[i, d, n], ring(axis, step))

    def ag_start(st):
        for n in (0, 1):
            for v in (0, 1):
                for d in (0, 1):
                    ag_copy(st, v, d, n).start()

    def ag_fwd(st):
        for v in (0, 1):
            for d in (0, 1):
                ag_copy(st, v, d, 0, True).wait_recv()
                ag_copy(st, v, d, 2).start()

    def ag_done(st):
        for n in (1, 2):
            for v in (0, 1):
                for d in (0, 1):
                    ag_copy(st, v, d, n, True).wait_recv()

    def tx_target(i):
        return zz(sg * i) if i != 2 else zz(-2 * sg)

    def tx_copy(i):
        z = tx_target(i)
        return remote(tok_ref.at[rows_of(z)], X.at[core, me], tx_s.at[i], tx_r.at[i], at(core, z))

    def frame(n):
        return zz(sg * n) if n < 4 else zz(-sg * (n - 3))

    def tp_copy(i):
        src = tok_ref.at[rows_of(me)] if i == 0 else X.at[core, frame(i)]
        return remote(src, X.at[core, frame(i)], tp_s.at[i], tp_r.at[i], partner)

    def ts_copy(n):
        return remote(X.at[core, frame(n)], X.at[core, frame(n)], ts_s.at[n], ts_r.at[n], sib)

    def tx_service(i):
        arrived(X.at[core, frame(i)], tx_s.at[i], tx_r.at[i])
        tp_copy(i).start()
        ts_copy(i).start()

    def tp_service(i):
        arrived(X.at[core, frame(4 + i)], tp_s.at[i], tp_r.at[i])
        ts_copy(4 + i).start()

    def da_copy(g, dc, df):
        k, z = other(dc), zz(df)
        src, dst = da_ref.at[rows_of(z), cols_of(k, z, g)], GA.at[g, core, me]
        if dc == 0 and df == 0:
            return pltpu.make_async_copy(src, dst, loc_sem.at[7 + g])
        return remote(src, dst, da_s.at[g, dc, df], da_r.at[g, dc, df], at(k, z))

    def da_wait(g):
        for dc in (0, 1):
            for df in range(8):
                if dc == 0 and df == 0:
                    da_copy(g, 0, 0).wait()
                else:
                    arrived(GA.at[g, other(dc), zz(-df)], da_s.at[g, dc, df], da_r.at[g, dc, df])

    near = (0, 1, 7, 2, 6, 3, 5, 4)
    CB[core] = jnp.full((8, 128), cnt_ref[0], jnp.int32)
    cb_copy = remote(CB.at[core], CB.at[core], cb_s.at[0], cb_r.at[0], sib)
    cb_copy.start()

    sts = ((0, 0), (1, 0), (0, 1), (1, 1))

    def da_begin(g):
        for df in near:
            for dc in (0, 1):
                da_copy(g, dc, df).start()

    for c in loc:
        c.wait()
    for t in range(4):
        zw_copy(t, 0).start()
    for i in (1, 2, 3):
        tx_copy(i).start()
    tp_copy(0).start()
    for t in range(4):
        zw_copy(t, 1).start()
    own_x.wait()
    ts_copy(0).start()
    for st in sts[:2]:
        zw_wait(*st)
        lt_start(st)
    lt_done(sts[0])
    ag_start(sts[0])
    tx_service(1)
    lt_done(sts[1])
    ag_start(sts[1])
    for st in sts[2:]:
        zw_wait(*st)
        lt_start(st)
    tp_service(0)
    ag_fwd(sts[0])
    tx_service(2)
    da_begin(0)
    for st in sts[2:]:
        lt_done(st)
    ag_start(sts[2])
    tp_service(1)
    tx_service(3)
    ag_fwd(sts[1])
    ag_start(sts[3])
    tp_service(2)
    tp_service(3)
    da_begin(1)
    for n in range(8):
        ref = X.at[1 - core, frame(n)]
        arrived(ref, ts_s.at[n], ts_r.at[n])

    def turn(i, _):
        x = X[:, :, :, pl.ds(pl.multiple_of(i * 384, 384), 384)].reshape(2 * F * Q, 384)
        XT[pl.ds(pl.multiple_of(i * 384, 384), 384), :] = x.T
        return 0

    ag_done(sts[0])
    arrived(CB.at[1 - core], cb_s.at[0], cb_r.at[0])

    row = lax.broadcasted_iota(jnp.int32, (128, 128), 0)
    col = lax.broadcasted_iota(jnp.int32, (128, 128), 1)
    same = jnp.bitwise_and(row, 15) == jnp.bitwise_and(col, 15)
    late = lax.shift_right_logical(col, 4)
    scale = HEAD_DIM ** -0.5

    def proj(st):
        x = X[...].reshape(2 * F * Q, D)
        cosv = cos_ref[...].reshape(1, F, 1, 128)
        sinv = sin_ref[...].reshape(1, F, 1, 128)
        pre = dot_nn(x, W[st[0], st[1]].reshape(D, T))
        for t in range(3):
            a = pre[:, t * 128:(t + 1) * 128]
            if t < 2:
                r = pltpu.roll(a, 64, 1).reshape(2, F, Q, 128)
                a = a.reshape(2, F, Q, 128) * cosv + r * sinv
            QKV[t] = a.reshape(2, F, Q, 128).astype(BF)

    def attend(st, c, b):
        g, u = st
        sl = slice(b * 16, (b + 1) * 16)
        hc = slice(u * 128, (u + 1) * 128)
        q = QKV[0, c, :, sl, :].reshape(128, 128)
        k = QKV[1, c, :, sl, :].reshape(128, 128)
        v = QKV[2, c, :, sl, :].reshape(128, 128)
        gr = GA[g, c, :, sl, hc].reshape(128, 128)
        live = same & (late < CB[c, 0:1, :])
        s = jnp.where(live, dot_nt(q, k) * scale, jnp.float32(-1e30))
        top = jnp.max(s, axis=1, keepdims=True)
        e = jnp.exp(s - top)
        prob = e / jnp.sum(e, axis=1, keepdims=True)
        pb = prob.astype(BF)
        O[g, c, :, sl, hc] = dot_nn(pb, v).astype(BF).reshape(8, 16, 128)
        dv = dot_tn(pb, gr)
        dpr = dot_nt(gr, v)
        inner = jnp.sum(prob * dpr, axis=1, keepdims=True)
        ds = prob * (dpr - inner) * scale
        hi = ds.astype(BF)
        lo = (ds - hi.astype(F32)).astype(BF)
        dq = dot_nn(hi, k) + dot_nn(lo, k)
        dk = dot_tn(hi, q) + dot_tn(lo, q)
        cosv = cos_ref[...].reshape(8, 1, 128)
        sinv = sin_ref[...].reshape(8, 1, 128)
        for t, val in ((0, dq), (1, dk)):
            r = pltpu.roll(val, 64, 1).reshape(8, 16, 128)
            un = val.reshape(8, 16, 128) * cosv - r * sinv
            DD[c, :, sl, t * 128:(t + 1) * 128] = un.astype(BF)
        DD[c, :, sl, 256:384] = dv.astype(BF).reshape(8, 16, 128)

    def at_cols(k, z, st):
        return pl.ds(pl.multiple_of(group_of(k, z, st[0]) * C + st[1] * 128, 128), 128)

    def at_copy(st, dc, df):
        g, u = st
        k, z = other(dc), zz(df)
        src = O.at[g, k, z, :, u * 128:(u + 1) * 128]
        dst = attn_ref.at[rows_of(me), at_cols(core, me, st)]
        if dc == 0 and df == 0:
            return pltpu.make_async_copy(src, dst, loc_sem.at[9 + 2 * g + u])
        return remote(src, dst, at_s.at[2 * g + u, dc, df], at_r.at[2 * g + u, dc, df], at(k, z))

    def at_begin(st):
        for df in near:
            for dc in (0, 1):
                at_copy(st, dc, df).start()

    def at_wait(st):
        i = 2 * st[0] + st[1]
        for dc in (0, 1):
            for df in range(8):
                if dc == 0 and df == 0:
                    at_copy(st, 0, 0).wait()
                else:
                    k, z = other(dc), zz(-df)
                    ref = attn_ref.at[rows_of(z), at_cols(k, z, st)]
                    arrived(ref, at_s.at[i, dc, df], at_r.at[i, dc, df])

    def grads(st):
        def body(i, _):
            x = XT[pl.ds(pl.multiple_of(i * 768, 768), 768), :]
            r = dot_nn(x, DD[...].reshape(2 * F * Q, T)).astype(BF)
            GS[st[0], st[1], i] = r.reshape(4, 2, 96, T)
            return 0

        lax.fori_loop(0, 4, body, 0)

    def partial(st):
        def body(i, _):
            w = W[st[0], st[1], i].reshape(768, T)
            r = dot_nt(DD[...].reshape(2 * F * Q, T), w).reshape(2, F, Q, 768)
            cs = pl.ds(pl.multiple_of(i * 768, 768), 768)
            if st == sts[0]:
                Y[:, :, :, cs] = r
            else:
                Y[:, :, :, cs] += r
            return 0

        lax.fori_loop(0, 4, body, 0)

    def rs_copy(st, v, d, n):
        g, u = st
        step = 1 if d == 0 else -1
        axis = axis_of(v, 1)
        p = m4(pos_of(axis) + step * (2 if n == 0 else 1))
        h = d if n != 1 else 1 - d
        i = g * 4 + u * 2 + v
        return remote(heavy(GS.at[g, u], v, p, h), HR.at[g, u, v, d, n],
                      rs_s.at[i, d, n], rs_r.at[i, d, n], ring(axis, step))

    def rs_arrived(st, v, d, n):
        g, u = st
        i = g * 4 + u * 2 + v
        arrived(HR.at[g, u, v, d, n], rs_s.at[i, d, n], rs_r.at[i, d, n])

    def rs_start(st):
        for n in (0, 1):
            for v in (0, 1):
                for d in (0, 1):
                    rs_copy(st, v, d, n).start()

    def rs_fwd(st):
        g, u = st
        for v in (0, 1):
            axis = axis_of(v, 1)
            for d in (0, 1):
                rs_arrived(st, v, d, 0)
                ref = heavy(GS.at[g, u], v, m4(pos_of(axis) + (1 if d == 0 else -1)), d)
                ref[...] = (ref[...].astype(F32) + HR[g, u, v, d, 0].astype(F32)).astype(BF)
                rs_copy(st, v, d, 2).start()

    def rl_copy(st, v, i):
        g, u = st
        axis = axis_of(v, 0)
        j = g * 4 + u * 2 + v
        return remote(R1.at[g, u, v, m4(pos_of(axis) + i)], LR.at[g, u, v, i - 1],
                      rl_s.at[j, i], rl_r.at[j, i], ring(axis, i))

    def rs_turn(st):
        g, u = st
        for v in (0, 1):
            axis = axis_of(v, 1)
            for n in (1, 2):
                for d in (0, 1):
                    rs_arrived(st, v, d, n)
            for h in (0, 1):
                own = heavy(GS.at[g, u], v, pos_of(axis), h)[...].astype(F32)
                first = HR[g, u, v, 0, 2 if h == 0 else 1].astype(F32)
                second = HR[g, u, v, 1, 1 if h == 0 else 2].astype(F32)
                R1[g, u, v, 2 * h:2 * h + 2] = (own + first + second).astype(BF)
            for i in (1, 3, 2):
                rl_copy(st, v, i).start()

    def zr_copy(st, k):
        g, u = st
        return remote(R2.at[g, u, k], ZR.at[u, quarter], zr_s.at[g, u, k],
                      zr_r.at[u, quarter], at(k, group_of(core, me, g)))

    def rs_last(st):
        g, u = st
        for v in (0, 1):
            for i in (1, 3, 2):
                rl_copy(st, v, i).wait_recv()
            own = R1[g, u, v, pos_of(axis_of(v, 0))].astype(F32)
            R2[g, u, v] = (own + LR[g, u, v, 0].astype(F32) + LR[g, u, v, 1].astype(F32)
                           + LR[g, u, v, 2].astype(F32)).astype(BF)
            zr_copy(st, v).start()

    def all_attend(st):
        for c in (0, 1):
            for b in (0, 1):
                attend(st, c, b)

    proj(sts[0])
    ag_fwd(sts[2])
    lax.fori_loop(0, 8, turn, 0)
    da_wait(0)
    all_attend(sts[0])
    grads(sts[0])
    rs_start(sts[0])
    at_begin(sts[0])
    partial(sts[0])

    ag_done(sts[1])
    proj(sts[1])
    ag_fwd(sts[3])
    da_wait(1)
    all_attend(sts[1])
    rs_fwd(sts[0])
    grads(sts[1])
    rs_start(sts[1])
    at_begin(sts[1])
    partial(sts[1])

    ag_done(sts[2])
    proj(sts[2])
    all_attend(sts[2])
    rs_fwd(sts[1])
    grads(sts[2])
    rs_start(sts[2])
    at_begin(sts[2])
    rs_turn(sts[0])
    partial(sts[2])

    ag_done(sts[3])
    proj(sts[3])
    all_attend(sts[3])
    rs_fwd(sts[2])
    partial(sts[3])

    def sy_copy(f):
        return remote(SYS.at[f], SYR.at[f], sy_s.at[f], sy_r.at[f], sib)

    for n in (4, 5, 6, 7, 1, 2, 3, 0):
        f = frame(n)
        SYS[f] = Y[1 - core, f].astype(BF)
        sy_copy(f).start()

    grads(sts[3])
    rs_start(sts[3])

    def own_sum(n):
        f = frame(n)
        sy_copy(f).wait_recv()
        return Y[core, f] + SYR[f].astype(F32)

    def pp_copy(i):
        return remote(PS.at[i], PR.at[i], pp_s.at[i], pp_r.at[i], partner)

    def td_copy(i):
        return remote(TD.at[i], dtok_ref.at[rows_of(me)], td_s.at[i], td_r.at[i], at(core, frame(i)))

    for i in (1, 2, 3, 0):
        PS[i] = own_sum(4 + i).astype(BF)
        pp_copy(i).start()
    rs_turn(sts[1])
    rs_last(sts[0])
    for i in (1, 2, 3, 0):
        part = own_sum(i)
        pp_copy(i).wait_recv()
        tot = (part + PR[i].astype(F32)).astype(BF)
        if i:
            TD[i] = tot
            td_copy(i).start()
        else:
            dtok_ref[rows_of(me), :] = tot
        if i == 1:
            rs_fwd(sts[3])
            rs_turn(sts[2])
        if i == 2:
            rs_last(sts[1])
            at_begin(sts[3])
        if i == 3:
            rs_last(sts[2])
    rs_turn(sts[3])
    rs_last(sts[3])

    for st in sts:
        at_wait(st)
    for i in (1, 2, 3):
        arrived(dtok_ref.at[rows_of(tx_target(i))], td_s.at[i], td_r.at[i])
    for u in (0, 1):
        for q in range(4):
            arrived(ZR.at[u, q], zr_s.at[0, 0, 0], zr_r.at[u, q])
        tot = (ZR[u, 0].astype(F32) + ZR[u, 1].astype(F32)
               + ZR[u, 2].astype(F32) + ZR[u, 3].astype(F32))
        for t, ref in enumerate((gq_ref, gk_ref, gv_ref)):
            ref[:, u * 128:(u + 1) * 128] = tot[:, t * 128:(t + 1) * 128]

    for st in sts:
        for v in (0, 1):
            for d in (0, 1):
                for n in range(3):
                    ag_copy(st, v, d, n).wait_send()
                    rs_copy(st, v, d, n).wait_send()
            for i in (1, 2, 3):
                lt_copy(st, v, i).wait_send()
                rl_copy(st, v, i).wait_send()
            zr_copy(st, v).wait_send()
        for dc in (0, 1):
            for df in range(8):
                if dc or df:
                    at_copy(st, dc, df).wait_send()
    for g in (0, 1):
        for dc in (0, 1):
            for df in range(8):
                if dc or df:
                    da_copy(g, dc, df).wait_send()
    for t in range(4):
        for u in (0, 1):
            zw_copy(t, u).wait_send()
    for i in range(4):
        tp_copy(i).wait_send()
        pp_copy(i).wait_send()
        if i:
            tx_copy(i).wait_send()
            td_copy(i).wait_send()
    cb_copy.wait_send()
    for n in range(8):
        ts_copy(n).wait_send()
        sy_copy(n).wait_send()


def place(*refs):
    sem = refs[10]
    copies = [pltpu.make_async_copy(refs[i], refs[5 + i], sem.at[i]) for i in range(5)]
    for c in copies:
        c.start()
    for c in copies:
        c.wait()


def place(*refs):
    src, dst, buf = refs[0:5], refs[5:10], refs[10:15]
    get, put = refs[15:17]
    first = [pltpu.make_async_copy(src[i], buf[i], get.at[i]) for i in range(5)]
    second = [pltpu.make_async_copy(buf[i], dst[i], put.at[i]) for i in range(5)]
    for c in first:
        c.start()
    for a, b in zip(first, second):
        a.wait()
        b.start()
    for c in second:
        c.wait()


def tables():
    half = HEAD_DIM // 2
    inv = 10000.0 ** (-(2.0 * np.arange(half, dtype=np.float32)) / HEAD_DIM)
    angle = np.arange(F, dtype=np.float32)[:, None] * inv[None, :].astype(np.float32)
    c, s = np.cos(angle), np.sin(angle)
    return (np.concatenate([c, c], 1).astype(np.float32),
            np.concatenate([-s, s], 1).astype(np.float32))


def on_device(tokens, d_attn, frame_counts, w_query, w_key, w_value):
    cosine, sine = tables()
    any_ = pl.BlockSpec(memory_space=pl.ANY)
    vmem = pl.BlockSpec(memory_space=pltpu.VMEM)
    smem = pl.BlockSpec(memory_space=pltpu.SMEM)
    dma = pltpu.SemaphoreType.DMA
    outs = pl.pallas_call(
        kernel,
        out_shape=(
            jax.ShapeDtypeStruct((S, F * C), BF),
            jax.ShapeDtypeStruct((S, D), BF),
            jax.ShapeDtypeStruct((96, C), F32),
            jax.ShapeDtypeStruct((96, C), F32),
            jax.ShapeDtypeStruct((96, C), F32),
        ),
        in_specs=[smem, any_, any_, any_, any_, any_, vmem, vmem],
        out_specs=(vmem,) * 5,
        scratch_shapes=[
            pltpu.VMEM((2, F, Q, D), BF),
            pltpu.VMEM((D, 2 * F * Q), BF),
            pltpu.VMEM((2, 96, T), BF),
            pltpu.VMEM((2, 2, 4, 4, 2, 96, T), BF),
            pltpu.VMEM((2, 2, F, Q, C), BF),
            pltpu.VMEM((3, 2, F, Q, 128), BF),
            pltpu.VMEM((2, F, Q, T), BF),
            pltpu.VMEM((2, 2, F, Q, C), BF),
            pltpu.VMEM((2, F, Q, D), F32),
            pltpu.VMEM((2, 2, 4, 4, 2, 96, T), BF),
            pltpu.VMEM((2, 2, 2, 2, 3, 2, 96, T), BF),
            pltpu.VMEM((2, 2, 2, 4, 96, T), BF),
            pltpu.VMEM((2, 2, 2, 3, 96, T), BF),
            pltpu.VMEM((2, 2, 2, 96, T), BF),
            pltpu.VMEM((2, 4, 96, T), BF),
            pltpu.VMEM((F, Q, D), BF),
            pltpu.VMEM((F, Q, D), BF),
            pltpu.VMEM((4, Q, D), BF),
            pltpu.VMEM((4, Q, D), BF),
            pltpu.VMEM((4, Q, D), BF),
            pltpu.VMEM((2, 8, 128), jnp.int32),
            dma((13,)),
            dma((4, 2)), dma((2, 2, 2)),
            dma((8, 2, 3)), dma((8, 2, 3)),
            dma((4,)), dma((4,)),
            dma((4,)), dma((4,)),
            dma((8,)), dma((8,)),
            dma((2, 2, 8)), dma((2, 2, 8)),
            dma((4, 2, 8)), dma((4, 2, 8)),
            dma((8, 2, 3)), dma((8, 2, 3)),
            dma((2, 2, 2)), dma((2, 4)),
            dma((8,)), dma((8,)),
            dma((4,)), dma((4,)),
            dma((4,)), dma((4,)),
            dma((1,)), dma((1,)),
            dma((8, 4)), dma((8, 4)),
            dma((8, 4)), dma((8, 4)),
        ],
        compiler_params=pltpu.CompilerParams(
            collective_id=0, has_side_effects=True, vmem_limit_bytes=62 * 1024 * 1024),
        name="temporal_attention",
    )(
        frame_counts, tokens.reshape(S, D),
        d_attn.reshape(S, F * C), w_query, w_key, w_value, jnp.asarray(cosine), jnp.asarray(sine),
    )
    shapes = tuple(jax.ShapeDtypeStruct(o.shape, o.dtype) for o in outs)
    outs = pl.pallas_call(
        place,
        out_shape=shapes,
        in_specs=[any_] * 5,
        out_specs=(any_,) * 5,
        scratch_shapes=[pltpu.VMEM(o.shape, o.dtype) for o in outs] + [dma((5,)), dma((5,))],
        compiler_params=pltpu.CompilerParams(vmem_limit_bytes=62 * 1024 * 1024),
        name="place",
    )(*outs)
    attn, dtok, gq, gk, gv = outs
    return attn.reshape(d_attn.shape), dtok.reshape(tokens.shape), gq, gk, gv


def solution(mesh):
    return jax.shard_map(
        on_device,
        mesh=mesh,
        in_specs=(
            P("dp", "seq", None, None),
            P("dp", "seq", None, None),
            P("dp"),
            P("dp", "seq"),
            P("dp", "seq"),
            P("dp", "seq"),
        ),
        out_specs=(
            P("dp", "seq", None, None),
            P("dp", "seq", None, None),
            P("dp", "seq"),
            P("dp", "seq"),
            P("dp", "seq"),
        ),
        check_vma=False,
    )
```

```python
import functools

import jax
import jax.numpy as jnp
import numpy as np
from jax import lax
from jax.experimental import pallas as pl
from jax.experimental.pallas import tpu as pltpu
from jax.sharding import PartitionSpec as P

HEAD_DIM = 128
F = 8
S = 128
D = 3072
C = 256
Q = 32
T = 3 * HEAD_DIM
MESH = pl.DeviceIdType.MESH
BF = jnp.bfloat16
F32 = jnp.float32
ZOFF = (1, -1, 3, -3)


def dot_nt(a, b):
    return lax.dot_general(a, b, (((1,), (1,)), ((), ())), preferred_element_type=F32)


def dot_tn(a, b):
    return lax.dot_general(a, b, (((0,), (0,)), ((), ())), preferred_element_type=F32)


def dot_nn(a, b):
    return jnp.dot(a, b, preferred_element_type=F32)


def kernel(
    cnt_ref, tok_ref, da_ref, wq_ref, wk_ref, wv_ref, cos_ref, sin_ref,
    attn_ref, dtok_ref, gq_ref, gk_ref, gv_ref,
    X, XT, PK, W, GA, QKV, DD, O, Y, GS, HR, R1, LR, R2, ZR, SYS, SYR, PS, PR, TD, CB,
    loc_sem, zw_s, zw_r, ag_s, ag_r, tx_s, tx_r, tp_s, tp_r, ts_s, ts_r, da_s, da_r,
    at_s, at_r, rs_s, rs_r, zr_s, zr_r, sy_s, sy_r, pp_s, pp_r, td_s, td_r, cb_s, cb_r, lt_s, lt_r, rl_s, rl_r,
):
    dp = lax.axis_index("dp")
    me = lax.axis_index("seq")
    core = lax.rem(dp, 2)
    chip = dp // 2
    cx = chip // 4
    cy = lax.rem(chip, 4)
    par = lax.rem(me, 2)
    sg = 2 * par - 1
    quarter = me // 2

    def zz(i):
        return lax.rem(me + (i + 16), 8)

    def m4(i):
        return lax.rem(i + 8, 4)

    def at(k, z):
        return (chip * 2 + k, z)

    def other(dc):
        return core if dc == 0 else 1 - core

    def rows_of(z):
        return pl.ds(pl.multiple_of((z // 2) * Q, Q), Q)

    def group_of(k, z, g):
        return (1 - lax.rem(z, 2)) + 2 * k + 4 * g

    def cols_of(k, z, g):
        return pl.ds(pl.multiple_of(group_of(k, z, g) * C, C), C)

    sib = at(1 - core, me)
    partner = at(core, zz(-sg))

    def remote(src, dst, ssem, rsem, dev):
        return pltpu.make_async_remote_copy(
            src_ref=src, dst_ref=dst, send_sem=ssem, recv_sem=rsem,
            device_id=dev, device_id_type=MESH,
        )

    def arrived(ref, ssem, rsem):
        remote(ref, ref, ssem, rsem, sib).wait_recv()

    loc = []
    for t, w in enumerate((wq_ref, wk_ref, wv_ref)):
        for u in (0, 1):
            loc.append(pltpu.make_async_copy(
                w.at[:, u * 128:(u + 1) * 128], PK.at[u, :, t * 128:(t + 1) * 128],
                loc_sem.at[2 * t + u]))
    own_x = pltpu.make_async_copy(tok_ref.at[rows_of(me)], X.at[core, me], loc_sem.at[6])
    for c in loc:
        c.start()
    own_x.start()

    bar = pltpu.get_barrier_semaphore()

    def greet(dev):
        pl.semaphore_signal(bar, inc=1, device_id=dev, device_id_type=MESH)

    def ring(axis, i):
        if axis == 0:
            return (m4(cx + i) * 8 + cy * 2 + core, me)
        return (cx * 8 + m4(cy + i) * 2 + core, me)

    for i in range(1, 8):
        greet(at(core, zz(i)))
        greet(at(1 - core, zz(i)))
    greet(sib)
    for axis in (0, 1):
        greet(ring(axis, 1))
        greet(ring(axis, -1))
        greet(ring(axis, 2))
    pl.semaphore_wait(bar, 21)

    def zw_copy(t, u):
        return remote(
            PK.at[u], W.at[me // 4, u, cx, cy, core], zw_s.at[t, u],
            zw_r.at[me // 4, u, core], at(lax.rem(me // 2, 2), zz(ZOFF[t])))

    def zw_wait(g, u):
        for k in (0, 1):
            arrived(W.at[g, u, cx, cy, k], zw_s.at[0, u], zw_r.at[g, u, k])

    def axis_of(v, ph):
        return v if ph == 0 else 1 - v

    def pos_of(axis):
        return cx if axis == 0 else cy

    def heavy(ref, v, p, h):
        return ref.at[2 * h:2 * h + 2, p, v] if v == 0 else ref.at[p, 2 * h:2 * h + 2, v]

    def light(ref, v, p):
        return ref.at[p, cy, v] if v == 0 else ref.at[cx, p, v]

    def lt_copy(st, v, i, recv=False):
        g, u = st
        axis = axis_of(v, 0)
        ref = light(W.at[g, u], v, m4(pos_of(axis) - (i if recv else 0)))
        j = g * 4 + u * 2 + v
        return remote(ref, ref, lt_s.at[j, i], lt_r.at[j, i], ring(axis, i))

    def lt_start(st):
        for i in (1, 3, 2):
            for v in (0, 1):
                lt_copy(st, v, i).start()

    def lt_done(st):
        for i in (1, 3, 2):
            for v in (0, 1):
                lt_copy(st, v, i, True).wait_recv()

    def ag_copy(st, v, d, n, recv=False):
        g, u = st
        step = 1 if d == 0 else -1
        axis = axis_of(v, 1)
        back = (1 if n == 2 else 0) + (1 if recv else 0)
        p = m4(pos_of(axis) - step * back)
        h = d if n != 1 else 1 - d
        ref = heavy(W.at[g, u], v, p, h)
        i = g * 4 + u * 2 + v
        return remote(ref, ref, ag_s.at[i, d, n], ag_r.at[i, d, n], ring(axis, step))

    def ag_start(st):
        for n in (0, 1):
            for v in (0, 1):
                for d in (0, 1):
                    ag_copy(st, v, d, n).start()

    def ag_fwd(st):
        for v in (0, 1):
            for d in (0, 1):
                ag_copy(st, v, d, 0, True).wait_recv()
                ag_copy(st, v, d, 2).start()

    def ag_done(st):
        for n in (1, 2):
            for v in (0, 1):
                for d in (0, 1):
                    ag_copy(st, v, d, n, True).wait_recv()

    def tx_target(i):
        return zz(sg * i) if i != 2 else zz(-2 * sg)

    def tx_copy(i):
        z = tx_target(i)
        return remote(tok_ref.at[rows_of(z)], X.at[core, me], tx_s.at[i], tx_r.at[i], at(core, z))

    def frame(n):
        return zz(sg * n) if n < 4 else zz(-sg * (n - 3))

    def tp_copy(i):
        src = tok_ref.at[rows_of(me)] if i == 0 else X.at[core, frame(i)]
        return remote(src, X.at[core, frame(i)], tp_s.at[i], tp_r.at[i], partner)

    def ts_copy(n):
        return remote(X.at[core, frame(n)], X.at[core, frame(n)], ts_s.at[n], ts_r.at[n], sib)

    def tx_service(i):
        arrived(X.at[core, frame(i)], tx_s.at[i], tx_r.at[i])
        tp_copy(i).start()
        ts_copy(i).start()

    def tp_service(i):
        arrived(X.at[core, frame(4 + i)], tp_s.at[i], tp_r.at[i])
        ts_copy(4 + i).start()

    def da_copy(g, dc, df):
        k, z = other(dc), zz(df)
        src, dst = da_ref.at[rows_of(z), cols_of(k, z, g)], GA.at[g, core, me]
        if dc == 0 and df == 0:
            return pltpu.make_async_copy(src, dst, loc_sem.at[7 + g])
        return remote(src, dst, da_s.at[g, dc, df], da_r.at[g, dc, df], at(k, z))

    def da_wait(g):
        for dc in (0, 1):
            for df in range(8):
                if dc == 0 and df == 0:
                    da_copy(g, 0, 0).wait()
                else:
                    arrived(GA.at[g, other(dc), zz(-df)], da_s.at[g, dc, df], da_r.at[g, dc, df])

    near = (0, 1, 7, 2, 6, 3, 5, 4)
    CB[core] = jnp.full((8, 128), cnt_ref[0], jnp.int32)
    cb_copy = remote(CB.at[core], CB.at[core], cb_s.at[0], cb_r.at[0], sib)
    cb_copy.start()

    sts = ((0, 0), (1, 0), (0, 1), (1, 1))

    def da_begin(g):
        for df in near:
            for dc in (0, 1):
                da_copy(g, dc, df).start()

    for c in loc:
        c.wait()
    for t in range(4):
        zw_copy(t, 0).start()
    for i in (1, 2, 3):
        tx_copy(i).start()
    tp_copy(0).start()
    own_x.wait()
    ts_copy(0).start()
    for st in sts[:2]:
        zw_wait(*st)
        lt_start(st)
    tx_service(1)
    lt_done(sts[0])
    ag_start(sts[0])
    for t in range(4):
        zw_copy(t, 1).start()
    tp_service(0)
    tx_service(2)
    lt_done(sts[1])
    ag_start(sts[1])
    tx_service(3)
    tp_service(1)
    ag_fwd(sts[0])
    da_begin(0)
    for st in sts[2:]:
        zw_wait(*st)
        lt_start(st)
    ag_fwd(sts[1])
    tp_service(2)
    for st in sts[2:]:
        lt_done(st)
        ag_start(st)
    tp_service(3)
    da_begin(1)
    for n in range(8):
        ref = X.at[1 - core, frame(n)]
        arrived(ref, ts_s.at[n], ts_r.at[n])

    def turn(i, _):
        x = X[:, :, :, pl.ds(pl.multiple_of(i * 384, 384), 384)].reshape(2 * F * Q, 384)
        XT[pl.ds(pl.multiple_of(i * 384, 384), 384), :] = x.T
        return 0

    ag_done(sts[0])
    arrived(CB.at[1 - core], cb_s.at[0], cb_r.at[0])

    row = lax.broadcasted_iota(jnp.int32, (128, 128), 0)
    col = lax.broadcasted_iota(jnp.int32, (128, 128), 1)
    same = jnp.bitwise_and(row, 15) == jnp.bitwise_and(col, 15)
    late = lax.shift_right_logical(col, 4)
    scale = HEAD_DIM ** -0.5

    def proj(st):
        x = X[...].reshape(2 * F * Q, D)
        cosv = cos_ref[...].reshape(1, F, 1, 128)
        sinv = sin_ref[...].reshape(1, F, 1, 128)
        pre = dot_nn(x, W[st[0], st[1]].reshape(D, T))
        for t in range(3):
            a = pre[:, t * 128:(t + 1) * 128]
            if t < 2:
                r = pltpu.roll(a, 64, 1).reshape(2, F, Q, 128)
                a = a.reshape(2, F, Q, 128) * cosv + r * sinv
            QKV[t] = a.reshape(2, F, Q, 128).astype(BF)

    def attend(st, c, b):
        g, u = st
        sl = slice(b * 16, (b + 1) * 16)
        hc = slice(u * 128, (u + 1) * 128)
        q = QKV[0, c, :, sl, :].reshape(128, 128)
        k = QKV[1, c, :, sl, :].reshape(128, 128)
        v = QKV[2, c, :, sl, :].reshape(128, 128)
        gr = GA[g, c, :, sl, hc].reshape(128, 128)
        live = same & (late < CB[c, 0:1, :])
        s = jnp.where(live, dot_nt(q, k) * scale, jnp.float32(-1e30))
        top = jnp.max(s, axis=1, keepdims=True)
        e = jnp.exp(s - top)
        prob = e / jnp.sum(e, axis=1, keepdims=True)
        pb = prob.astype(BF)
        O[g, c, :, sl, hc] = dot_nn(pb, v).astype(BF).reshape(8, 16, 128)
        dv = dot_tn(pb, gr)
        dpr = dot_nt(gr, v)
        inner = jnp.sum(prob * dpr, axis=1, keepdims=True)
        ds = prob * (dpr - inner) * scale
        hi = ds.astype(BF)
        lo = (ds - hi.astype(F32)).astype(BF)
        dq = dot_nn(hi, k) + dot_nn(lo, k)
        dk = dot_tn(hi, q) + dot_tn(lo, q)
        cosv = cos_ref[...].reshape(8, 1, 128)
        sinv = sin_ref[...].reshape(8, 1, 128)
        for t, val in ((0, dq), (1, dk)):
            r = pltpu.roll(val, 64, 1).reshape(8, 16, 128)
            un = val.reshape(8, 16, 128) * cosv - r * sinv
            DD[g, u, c, :, sl, t * 128:(t + 1) * 128] = un.astype(BF)
        DD[g, u, c, :, sl, 256:384] = dv.astype(BF).reshape(8, 16, 128)

    def at_cols(k, z, st):
        return pl.ds(pl.multiple_of(group_of(k, z, st[0]) * C + st[1] * 128, 128), 128)

    def at_copy(st, dc, df):
        g, u = st
        k, z = other(dc), zz(df)
        src = O.at[g, k, z, :, u * 128:(u + 1) * 128]
        dst = attn_ref.at[rows_of(me), at_cols(core, me, st)]
        if dc == 0 and df == 0:
            return pltpu.make_async_copy(src, dst, loc_sem.at[9 + 2 * g + u])
        return remote(src, dst, at_s.at[2 * g + u, dc, df], at_r.at[2 * g + u, dc, df], at(k, z))

    def at_begin(st):
        for df in near:
            for dc in (0, 1):
                at_copy(st, dc, df).start()

    def at_wait(st):
        i = 2 * st[0] + st[1]
        for dc in (0, 1):
            for df in range(8):
                if dc == 0 and df == 0:
                    at_copy(st, 0, 0).wait()
                else:
                    k, z = other(dc), zz(-df)
                    ref = attn_ref.at[rows_of(z), at_cols(k, z, st)]
                    arrived(ref, at_s.at[i, dc, df], at_r.at[i, dc, df])

    def grads(st):
        def body(i, _):
            x = XT[pl.ds(pl.multiple_of(i * 768, 768), 768), :]
            r = dot_nn(x, DD[st[0], st[1]].reshape(2 * F * Q, T)).astype(BF)
            GS[st[0], st[1], i] = r.reshape(4, 2, 96, T)
            return 0

        lax.fori_loop(0, 4, body, 0)

    def sy_copy(i):
        cs = pl.ds(pl.multiple_of(i * 768, 768), 768)
        return remote(SYS.at[:, :, cs], SYR.at[:, :, cs], sy_s.at[i], sy_r.at[i], sib)

    def partial(c, out, send):
        def body(i, _):
            w = jnp.concatenate([W[g, u, i].reshape(768, T) for g, u in sts], axis=1)
            d = jnp.concatenate([DD[g, u, c].reshape(F * Q, T) for g, u in sts], axis=1)
            cs = pl.ds(pl.multiple_of(i * 768, 768), 768)
            out[:, :, cs] = dot_nt(d, w).reshape(F, Q, 768).astype(out.dtype)
            if send:
                sy_copy(i).start()
            return 0

        lax.fori_loop(0, 4, body, 0)

    def rs_copy(st, v, d, n):
        g, u = st
        step = 1 if d == 0 else -1
        axis = axis_of(v, 1)
        p = m4(pos_of(axis) + step * (2 if n == 0 else 1))
        h = d if n != 1 else 1 - d
        i = g * 4 + u * 2 + v
        return remote(heavy(GS.at[g, u], v, p, h), HR.at[g, u, v, d, n],
                      rs_s.at[i, d, n], rs_r.at[i, d, n], ring(axis, step))

    def rs_arrived(st, v, d, n):
        g, u = st
        i = g * 4 + u * 2 + v
        arrived(HR.at[g, u, v, d, n], rs_s.at[i, d, n], rs_r.at[i, d, n])

    def rs_start(st):
        for n in (0, 1):
            for v in (0, 1):
                for d in (0, 1):
                    rs_copy(st, v, d, n).start()

    def rs_fwd(st):
        g, u = st
        for v in (0, 1):
            axis = axis_of(v, 1)
            for d in (0, 1):
                rs_arrived(st, v, d, 0)
                ref = heavy(GS.at[g, u], v, m4(pos_of(axis) + (1 if d == 0 else -1)), d)
                ref[...] = (ref[...].astype(F32) + HR[g, u, v, d, 0].astype(F32)).astype(BF)
                rs_copy(st, v, d, 2).start()

    def rl_copy(st, v, i):
        g, u = st
        axis = axis_of(v, 0)
        j = g * 4 + u * 2 + v
        return remote(R1.at[g, u, v, m4(pos_of(axis) + i)], LR.at[g, u, v, i - 1],
                      rl_s.at[j, i], rl_r.at[j, i], ring(axis, i))

    def rs_turn(st):
        g, u = st
        for v in (0, 1):
            axis = axis_of(v, 1)
            for n in (1, 2):
                for d in (0, 1):
                    rs_arrived(st, v, d, n)
            for h in (0, 1):
                own = heavy(GS.at[g, u], v, pos_of(axis), h)[...].astype(F32)
                first = HR[g, u, v, 0, 2 if h == 0 else 1].astype(F32)
                second = HR[g, u, v, 1, 1 if h == 0 else 2].astype(F32)
                R1[g, u, v, 2 * h:2 * h + 2] = (own + first + second).astype(BF)
            for i in (1, 3, 2):
                rl_copy(st, v, i).start()

    def zr_copy(st, k):
        g, u = st
        return remote(R2.at[g, u, k], ZR.at[u, quarter], zr_s.at[g, u, k],
                      zr_r.at[u, quarter], at(k, group_of(core, me, g)))

    def rs_last(st):
        g, u = st
        for v in (0, 1):
            for i in (1, 3, 2):
                rl_copy(st, v, i).wait_recv()
            own = R1[g, u, v, pos_of(axis_of(v, 0))].astype(F32)
            R2[g, u, v] = (own + LR[g, u, v, 0].astype(F32) + LR[g, u, v, 1].astype(F32)
                           + LR[g, u, v, 2].astype(F32)).astype(BF)
            zr_copy(st, v).start()

    def all_attend(st):
        for c in (0, 1):
            for b in (0, 1):
                attend(st, c, b)

    proj(sts[0])
    ag_fwd(sts[2])
    lax.fori_loop(0, 8, turn, 0)
    da_wait(0)
    all_attend(sts[0])
    grads(sts[0])
    ag_fwd(sts[3])
    rs_start(sts[0])
    at_begin(sts[0])

    ag_done(sts[1])
    proj(sts[1])
    da_wait(1)
    all_attend(sts[1])
    grads(sts[1])
    rs_start(sts[1])
    at_begin(sts[1])
    rs_fwd(sts[0])

    ag_done(sts[2])
    proj(sts[2])
    all_attend(sts[2])
    grads(sts[2])
    rs_start(sts[2])
    at_begin(sts[2])
    rs_fwd(sts[1])

    ag_done(sts[3])
    proj(sts[3])
    all_attend(sts[3])
    at_begin(sts[3])

    partial(1 - core, SYS, True)
    rs_turn(sts[0])
    rs_fwd(sts[2])
    partial(core, Y, False)
    for i in range(4):
        sy_copy(i).wait_recv()

    def own_sum(n):
        f = frame(n)
        return Y[f] + SYR[f].astype(F32)

    def pp_copy(i):
        return remote(PS.at[i], PR.at[i], pp_s.at[i], pp_r.at[i], partner)

    def td_copy(i):
        return remote(TD.at[i], dtok_ref.at[rows_of(me)], td_s.at[i], td_r.at[i], at(core, frame(i)))

    for i in (1, 2, 3, 0):
        PS[i] = own_sum(4 + i).astype(BF)
        pp_copy(i).start()
    grads(sts[3])
    rs_start(sts[3])
    rs_turn(sts[1])
    rs_last(sts[0])

    def deliver(i):
        part = own_sum(i)
        pp_copy(i).wait_recv()
        tot = (part + PR[i].astype(F32)).astype(BF)
        if i:
            TD[i] = tot
            td_copy(i).start()
        else:
            dtok_ref[rows_of(me), :] = tot

    deliver(1)
    rs_fwd(sts[3])
    deliver(2)
    rs_turn(sts[2])
    rs_last(sts[1])
    deliver(3)
    rs_turn(sts[3])
    rs_last(sts[2])
    deliver(0)
    rs_last(sts[3])

    for st in sts:
        at_wait(st)
    for i in (1, 2, 3):
        arrived(dtok_ref.at[rows_of(tx_target(i))], td_s.at[i], td_r.at[i])
    for u in (0, 1):
        for q in range(4):
            arrived(ZR.at[u, q], zr_s.at[0, 0, 0], zr_r.at[u, q])
        tot = (ZR[u, 0].astype(F32) + ZR[u, 1].astype(F32)
               + ZR[u, 2].astype(F32) + ZR[u, 3].astype(F32))
        for t, ref in enumerate((gq_ref, gk_ref, gv_ref)):
            ref[:, u * 128:(u + 1) * 128] = tot[:, t * 128:(t + 1) * 128]

    for st in sts:
        for v in (0, 1):
            for d in (0, 1):
                for n in range(3):
                    ag_copy(st, v, d, n).wait_send()
                    rs_copy(st, v, d, n).wait_send()
            for i in (1, 2, 3):
                lt_copy(st, v, i).wait_send()
                rl_copy(st, v, i).wait_send()
            zr_copy(st, v).wait_send()
        for dc in (0, 1):
            for df in range(8):
                if dc or df:
                    at_copy(st, dc, df).wait_send()
    for g in (0, 1):
        for dc in (0, 1):
            for df in range(8):
                if dc or df:
                    da_copy(g, dc, df).wait_send()
    for t in range(4):
        for u in (0, 1):
            zw_copy(t, u).wait_send()
    for i in range(4):
        tp_copy(i).wait_send()
        pp_copy(i).wait_send()
        sy_copy(i).wait_send()
        if i:
            tx_copy(i).wait_send()
            td_copy(i).wait_send()
    cb_copy.wait_send()
    for n in range(8):
        ts_copy(n).wait_send()


def place(*refs):
    sem = refs[10]
    copies = [pltpu.make_async_copy(refs[i], refs[5 + i], sem.at[i]) for i in range(5)]
    for c in copies:
        c.start()
    for c in copies:
        c.wait()


def place(*refs):
    src, dst, buf = refs[0:5], refs[5:10], refs[10:15]
    get, put = refs[15:17]
    first = [pltpu.make_async_copy(src[i], buf[i], get.at[i]) for i in range(5)]
    second = [pltpu.make_async_copy(buf[i], dst[i], put.at[i]) for i in range(5)]
    for c in first:
        c.start()
    for a, b in zip(first, second):
        a.wait()
        b.start()
    for c in second:
        c.wait()


def tables():
    half = HEAD_DIM // 2
    inv = 10000.0 ** (-(2.0 * np.arange(half, dtype=np.float32)) / HEAD_DIM)
    angle = np.arange(F, dtype=np.float32)[:, None] * inv[None, :].astype(np.float32)
    c, s = np.cos(angle), np.sin(angle)
    return (np.concatenate([c, c], 1).astype(np.float32),
            np.concatenate([-s, s], 1).astype(np.float32))


def on_device(tokens, d_attn, frame_counts, w_query, w_key, w_value):
    cosine, sine = tables()
    any_ = pl.BlockSpec(memory_space=pl.ANY)
    vmem = pl.BlockSpec(memory_space=pltpu.VMEM)
    smem = pl.BlockSpec(memory_space=pltpu.SMEM)
    dma = pltpu.SemaphoreType.DMA
    outs = pl.pallas_call(
        kernel,
        out_shape=(
            jax.ShapeDtypeStruct((S, F * C), BF),
            jax.ShapeDtypeStruct((S, D), BF),
            jax.ShapeDtypeStruct((96, C), F32),
            jax.ShapeDtypeStruct((96, C), F32),
            jax.ShapeDtypeStruct((96, C), F32),
        ),
        in_specs=[smem, any_, any_, any_, any_, any_, vmem, vmem],
        out_specs=(vmem,) * 5,
        scratch_shapes=[
            pltpu.VMEM((2, F, Q, D), BF),
            pltpu.VMEM((D, 2 * F * Q), BF),
            pltpu.VMEM((2, 96, T), BF),
            pltpu.VMEM((2, 2, 4, 4, 2, 96, T), BF),
            pltpu.VMEM((2, 2, F, Q, C), BF),
            pltpu.VMEM((3, 2, F, Q, 128), BF),
            pltpu.VMEM((2, 2, 2, F, Q, T), BF),
            pltpu.VMEM((2, 2, F, Q, C), BF),
            pltpu.VMEM((F, Q, D), F32),
            pltpu.VMEM((2, 2, 4, 4, 2, 96, T), BF),
            pltpu.VMEM((2, 2, 2, 2, 3, 2, 96, T), BF),
            pltpu.VMEM((2, 2, 2, 4, 96, T), BF),
            pltpu.VMEM((2, 2, 2, 3, 96, T), BF),
            pltpu.VMEM((2, 2, 2, 96, T), BF),
            pltpu.VMEM((2, 4, 96, T), BF),
            pltpu.VMEM((F, Q, D), BF),
            pltpu.VMEM((F, Q, D), BF),
            pltpu.VMEM((4, Q, D), BF),
            pltpu.VMEM((4, Q, D), BF),
            pltpu.VMEM((4, Q, D), BF),
            pltpu.VMEM((2, 8, 128), jnp.int32),
            dma((13,)),
            dma((4, 2)), dma((2, 2, 2)),
            dma((8, 2, 3)), dma((8, 2, 3)),
            dma((4,)), dma((4,)),
            dma((4,)), dma((4,)),
            dma((8,)), dma((8,)),
            dma((2, 2, 8)), dma((2, 2, 8)),
            dma((4, 2, 8)), dma((4, 2, 8)),
            dma((8, 2, 3)), dma((8, 2, 3)),
            dma((2, 2, 2)), dma((2, 4)),
            dma((8,)), dma((8,)),
            dma((4,)), dma((4,)),
            dma((4,)), dma((4,)),
            dma((1,)), dma((1,)),
            dma((8, 4)), dma((8, 4)),
            dma((8, 4)), dma((8, 4)),
        ],
        compiler_params=pltpu.CompilerParams(
            collective_id=0, has_side_effects=True, vmem_limit_bytes=62 * 1024 * 1024),
        name="temporal_attention",
    )(
        frame_counts, tokens.reshape(S, D),
        d_attn.reshape(S, F * C), w_query, w_key, w_value, jnp.asarray(cosine), jnp.asarray(sine),
    )
    shapes = tuple(jax.ShapeDtypeStruct(o.shape, o.dtype) for o in outs)
    outs = pl.pallas_call(
        place,
        out_shape=shapes,
        in_specs=[any_] * 5,
        out_specs=(any_,) * 5,
        scratch_shapes=[pltpu.VMEM(o.shape, o.dtype) for o in outs] + [dma((5,)), dma((5,))],
        compiler_params=pltpu.CompilerParams(vmem_limit_bytes=62 * 1024 * 1024),
        name="place",
    )(*outs)
    attn, dtok, gq, gk, gv = outs
    return attn.reshape(d_attn.shape), dtok.reshape(tokens.shape), gq, gk, gv


def solution(mesh):
    return jax.shard_map(
        on_device,
        mesh=mesh,
        in_specs=(
            P("dp", "seq", None, None),
            P("dp", "seq", None, None),
            P("dp"),
            P("dp", "seq"),
            P("dp", "seq"),
            P("dp", "seq"),
        ),
        out_specs=(
            P("dp", "seq", None, None),
            P("dp", "seq", None, None),
            P("dp", "seq"),
            P("dp", "seq"),
            P("dp", "seq"),
        ),
        check_vma=False,
    )
```

```python
import functools

import jax
import jax.numpy as jnp
import numpy as np
from jax import lax
from jax.experimental import pallas as pl
from jax.experimental.pallas import tpu as pltpu
from jax.sharding import PartitionSpec as P

HEAD_DIM = 128
F = 8
S = 128
D = 3072
C = 256
Q = 32
T = 3 * HEAD_DIM
MESH = pl.DeviceIdType.MESH
BF = jnp.bfloat16
F32 = jnp.float32
ZOFF = (1, -1, 3, -3)


def dot_nt(a, b):
    return lax.dot_general(a, b, (((1,), (1,)), ((), ())), preferred_element_type=F32)


def dot_tn(a, b):
    return lax.dot_general(a, b, (((0,), (0,)), ((), ())), preferred_element_type=F32)


def dot_nn(a, b):
    return jnp.dot(a, b, preferred_element_type=F32)


def kernel(
    cnt_ref, tok_ref, da_ref, wq_ref, wk_ref, wv_ref, cos_ref, sin_ref,
    attn_ref, dtok_ref, gq_ref, gk_ref, gv_ref,
    X, XT, PK, W, GA, QKV, DD, O, Y, GS, HR, R1, LR, R2, ZR, SYS, SYR, PS, PR, TD, CB,
    loc_sem, zw_s, zw_r, ag_s, ag_r, tx_s, tx_r, tp_s, tp_r, ts_s, ts_r, da_s, da_r,
    at_s, at_r, rs_s, rs_r, zr_s, zr_r, sy_s, sy_r, pp_s, pp_r, td_s, td_r, cb_s, cb_r, lt_s, lt_r, rl_s, rl_r,
):
    dp = lax.axis_index("dp")
    me = lax.axis_index("seq")
    core = lax.rem(dp, 2)
    chip = dp // 2
    cx = chip // 4
    cy = lax.rem(chip, 4)
    par = lax.rem(me, 2)
    sg = 2 * par - 1
    quarter = me // 2

    def zz(i):
        return lax.rem(me + (i + 16), 8)

    def m4(i):
        return lax.rem(i + 8, 4)

    def at(k, z):
        return (chip * 2 + k, z)

    def other(dc):
        return core if dc == 0 else 1 - core

    def rows_of(z):
        return pl.ds(pl.multiple_of((z // 2) * Q, Q), Q)

    def group_of(k, z, g):
        return (1 - lax.rem(z, 2)) + 2 * k + 4 * g

    def cols_of(k, z, g):
        return pl.ds(pl.multiple_of(group_of(k, z, g) * C, C), C)

    sib = at(1 - core, me)
    partner = at(core, zz(-sg))

    def remote(src, dst, ssem, rsem, dev):
        return pltpu.make_async_remote_copy(
            src_ref=src, dst_ref=dst, send_sem=ssem, recv_sem=rsem,
            device_id=dev, device_id_type=MESH,
        )

    def arrived(ref, ssem, rsem):
        remote(ref, ref, ssem, rsem, sib).wait_recv()

    loc = []
    for t, w in enumerate((wq_ref, wk_ref, wv_ref)):
        for u in (0, 1):
            loc.append(pltpu.make_async_copy(
                w.at[:, u * 128:(u + 1) * 128], PK.at[u, :, t * 128:(t + 1) * 128],
                loc_sem.at[2 * t + u]))
    own_x = pltpu.make_async_copy(tok_ref.at[rows_of(me)], X.at[core, me], loc_sem.at[6])
    for c in loc:
        c.start()
    own_x.start()

    bar = pltpu.get_barrier_semaphore()

    def greet(dev):
        pl.semaphore_signal(bar, inc=1, device_id=dev, device_id_type=MESH)

    def ring(axis, i):
        if axis == 0:
            return (m4(cx + i) * 8 + cy * 2 + core, me)
        return (cx * 8 + m4(cy + i) * 2 + core, me)

    for i in range(1, 8):
        greet(at(core, zz(i)))
        greet(at(1 - core, zz(i)))
    greet(sib)
    for axis in (0, 1):
        greet(ring(axis, 1))
        greet(ring(axis, -1))
        greet(ring(axis, 2))
    pl.semaphore_wait(bar, 21)

    def zw_copy(t, u):
        return remote(
            PK.at[u], W.at[me // 4, u, cx, cy, core], zw_s.at[t, u],
            zw_r.at[me // 4, u, core], at(lax.rem(me // 2, 2), zz(ZOFF[t])))

    def zw_wait(g, u):
        for k in (0, 1):
            arrived(W.at[g, u, cx, cy, k], zw_s.at[0, u], zw_r.at[g, u, k])

    def axis_of(v, ph):
        return v if ph == 0 else 1 - v

    def pos_of(axis):
        return cx if axis == 0 else cy

    def heavy(ref, v, p, h):
        return ref.at[2 * h:2 * h + 2, p, v] if v == 0 else ref.at[p, 2 * h:2 * h + 2, v]

    def light(ref, v, p):
        return ref.at[p, cy, v] if v == 0 else ref.at[cx, p, v]

    def lt_copy(st, v, i, recv=False):
        g, u = st
        axis = axis_of(v, 0)
        ref = light(W.at[g, u], v, m4(pos_of(axis) - (i if recv else 0)))
        j = g * 4 + u * 2 + v
        return remote(ref, ref, lt_s.at[j, i], lt_r.at[j, i], ring(axis, i))

    def lt_start(st):
        for i in (1, 3, 2):
            for v in (0, 1):
                lt_copy(st, v, i).start()

    def lt_done(st):
        for i in (1, 3, 2):
            for v in (0, 1):
                lt_copy(st, v, i, True).wait_recv()

    def ag_copy(st, v, d, n, recv=False):
        g, u = st
        step = 1 if d == 0 else -1
        axis = axis_of(v, 1)
        back = (1 if n == 2 else 0) + (1 if recv else 0)
        p = m4(pos_of(axis) - step * back)
        h = d if n != 1 else 1 - d
        ref = heavy(W.at[g, u], v, p, h)
        i = g * 4 + u * 2 + v
        return remote(ref, ref, ag_s.at[i, d, n], ag_r.at[i, d, n], ring(axis, step))

    def ag_start(st):
        for n in (0, 1):
            for v in (0, 1):
                for d in (0, 1):
                    ag_copy(st, v, d, n).start()

    def ag_fwd(st):
        for v in (0, 1):
            for d in (0, 1):
                ag_copy(st, v, d, 0, True).wait_recv()
                ag_copy(st, v, d, 2).start()

    def ag_done(st):
        for n in (1, 2):
            for v in (0, 1):
                for d in (0, 1):
                    ag_copy(st, v, d, n, True).wait_recv()

    def tx_target(i):
        return zz(sg * i) if i != 2 else zz(-2 * sg)

    def tx_copy(i):
        z = tx_target(i)
        return remote(tok_ref.at[rows_of(z)], X.at[core, me], tx_s.at[i], tx_r.at[i], at(core, z))

    def frame(n):
        return zz(sg * n) if n < 4 else zz(-sg * (n - 3))

    def tp_copy(i):
        src = tok_ref.at[rows_of(me)] if i == 0 else X.at[core, frame(i)]
        return remote(src, X.at[core, frame(i)], tp_s.at[i], tp_r.at[i], partner)

    def ts_copy(n):
        return remote(X.at[core, frame(n)], X.at[core, frame(n)], ts_s.at[n], ts_r.at[n], sib)

    def tx_service(i):
        arrived(X.at[core, frame(i)], tx_s.at[i], tx_r.at[i])
        tp_copy(i).start()
        ts_copy(i).start()

    def tp_service(i):
        arrived(X.at[core, frame(4 + i)], tp_s.at[i], tp_r.at[i])
        ts_copy(4 + i).start()

    def da_copy(g, dc, df):
        k, z = other(dc), zz(df)
        src, dst = da_ref.at[rows_of(z), cols_of(k, z, g)], GA.at[g, core, me]
        if dc == 0 and df == 0:
            return pltpu.make_async_copy(src, dst, loc_sem.at[7 + g])
        return remote(src, dst, da_s.at[g, dc, df], da_r.at[g, dc, df], at(k, z))

    def da_wait(g):
        for dc in (0, 1):
            for df in range(8):
                if dc == 0 and df == 0:
                    da_copy(g, 0, 0).wait()
                else:
                    arrived(GA.at[g, other(dc), zz(-df)], da_s.at[g, dc, df], da_r.at[g, dc, df])

    near = (0, 1, 7, 2, 6, 3, 5, 4)
    CB[core] = jnp.full((8, 128), cnt_ref[0], jnp.int32)
    cb_copy = remote(CB.at[core], CB.at[core], cb_s.at[0], cb_r.at[0], sib)
    cb_copy.start()

    sts = ((0, 0), (1, 0), (0, 1), (1, 1))

    def da_begin(g):
        for df in near:
            for dc in (0, 1):
                da_copy(g, dc, df).start()

    for c in loc:
        c.wait()
    for t in range(4):
        zw_copy(t, 0).start()
    for i in (1, 2, 3):
        tx_copy(i).start()
    tp_copy(0).start()
    own_x.wait()
    ts_copy(0).start()
    for st in sts[:2]:
        zw_wait(*st)
        lt_start(st)
    tx_service(1)
    lt_done(sts[0])
    ag_start(sts[0])
    for t in range(4):
        zw_copy(t, 1).start()
    tp_service(0)
    tx_service(2)
    lt_done(sts[1])
    ag_start(sts[1])
    tx_service(3)
    tp_service(1)
    ag_fwd(sts[0])
    da_begin(0)
    for st in sts[2:]:
        zw_wait(*st)
        lt_start(st)
    ag_fwd(sts[1])
    tp_service(2)
    for st in sts[2:]:
        lt_done(st)
        ag_start(st)
    tp_service(3)
    da_begin(1)
    for n in range(8):
        ref = X.at[1 - core, frame(n)]
        arrived(ref, ts_s.at[n], ts_r.at[n])

    def turn(i, _):
        x = X[:, :, :, pl.ds(pl.multiple_of(i * 384, 384), 384)].reshape(2 * F * Q, 384)
        XT[pl.ds(pl.multiple_of(i * 384, 384), 384), :] = x.T
        return 0

    ag_done(sts[0])
    arrived(CB.at[1 - core], cb_s.at[0], cb_r.at[0])

    row = lax.broadcasted_iota(jnp.int32, (128, 128), 0)
    col = lax.broadcasted_iota(jnp.int32, (128, 128), 1)
    same = jnp.bitwise_and(row, 15) == jnp.bitwise_and(col, 15)
    late = lax.shift_right_logical(col, 4)
    scale = HEAD_DIM ** -0.5

    def proj(st):
        x = X[...].reshape(2 * F * Q, D)
        cosv = cos_ref[...].reshape(1, F, 1, 128)
        sinv = sin_ref[...].reshape(1, F, 1, 128)
        pre = dot_nn(x, W[st[0], st[1]].reshape(D, T))
        for t in range(3):
            a = pre[:, t * 128:(t + 1) * 128]
            if t < 2:
                r = pltpu.roll(a, 64, 1).reshape(2, F, Q, 128)
                a = a.reshape(2, F, Q, 128) * cosv + r * sinv
            QKV[t] = a.reshape(2, F, Q, 128).astype(BF)

    def attend(st, c, b):
        g, u = st
        sl = slice(b * 16, (b + 1) * 16)
        hc = slice(u * 128, (u + 1) * 128)
        q = QKV[0, c, :, sl, :].reshape(128, 128)
        k = QKV[1, c, :, sl, :].reshape(128, 128)
        v = QKV[2, c, :, sl, :].reshape(128, 128)
        gr = GA[g, c, :, sl, hc].reshape(128, 128)
        live = same & (late < CB[c, 0:1, :])
        s = jnp.where(live, dot_nt(q, k) * scale, jnp.float32(-1e30))
        top = jnp.max(s, axis=1, keepdims=True)
        e = jnp.exp(s - top)
        prob = e / jnp.sum(e, axis=1, keepdims=True)
        pb = prob.astype(BF)
        O[g, c, :, sl, hc] = dot_nn(pb, v).astype(BF).reshape(8, 16, 128)
        dv = dot_tn(pb, gr)
        dpr = dot_nt(gr, v)
        inner = jnp.sum(prob * dpr, axis=1, keepdims=True)
        ds = prob * (dpr - inner) * scale
        hi = ds.astype(BF)
        lo = (ds - hi.astype(F32)).astype(BF)
        dq = dot_nn(hi, k) + dot_nn(lo, k)
        dk = dot_tn(hi, q) + dot_tn(lo, q)
        cosv = cos_ref[...].reshape(8, 1, 128)
        sinv = sin_ref[...].reshape(8, 1, 128)
        for t, val in ((0, dq), (1, dk)):
            r = pltpu.roll(val, 64, 1).reshape(8, 16, 128)
            un = val.reshape(8, 16, 128) * cosv - r * sinv
            DD[g, u, c, :, sl, t * 128:(t + 1) * 128] = un.astype(BF)
        DD[g, u, c, :, sl, 256:384] = dv.astype(BF).reshape(8, 16, 128)

    def at_cols(k, z, st):
        return pl.ds(pl.multiple_of(group_of(k, z, st[0]) * C + st[1] * 128, 128), 128)

    def at_copy(st, dc, df):
        g, u = st
        k, z = other(dc), zz(df)
        src = O.at[g, k, z, :, u * 128:(u + 1) * 128]
        dst = attn_ref.at[rows_of(me), at_cols(core, me, st)]
        if dc == 0 and df == 0:
            return pltpu.make_async_copy(src, dst, loc_sem.at[9 + 2 * g + u])
        return remote(src, dst, at_s.at[2 * g + u, dc, df], at_r.at[2 * g + u, dc, df], at(k, z))

    def at_begin(st):
        for df in near:
            for dc in (0, 1):
                at_copy(st, dc, df).start()

    def at_wait(st):
        i = 2 * st[0] + st[1]
        for dc in (0, 1):
            for df in range(8):
                if dc == 0 and df == 0:
                    at_copy(st, 0, 0).wait()
                else:
                    k, z = other(dc), zz(-df)
                    ref = attn_ref.at[rows_of(z), at_cols(k, z, st)]
                    arrived(ref, at_s.at[i, dc, df], at_r.at[i, dc, df])

    def grads(st):
        def body(i, _):
            x = XT[pl.ds(pl.multiple_of(i * 768, 768), 768), :]
            r = dot_nn(x, DD[st[0], st[1]].reshape(2 * F * Q, T)).astype(BF)
            GS[st[0], st[1], i] = r.reshape(4, 2, 96, T)
            return 0

        lax.fori_loop(0, 4, body, 0)

    def sy_copy(i):
        cs = pl.ds(pl.multiple_of(i * 768, 768), 768)
        return remote(SYS.at[:, :, cs], SYR.at[:, :, cs], sy_s.at[i], sy_r.at[i], sib)

    def partial_first():
        def body(i, _):
            w = jnp.concatenate([W[g, u, i].reshape(768, T) for g, u in sts[:2]], axis=1)
            d = jnp.concatenate([DD[g, u].reshape(2 * F * Q, T) for g, u in sts[:2]], axis=1)
            cs = pl.ds(pl.multiple_of(i * 768, 768), 768)
            Y[:, :, :, cs] = dot_nt(d, w).reshape(2, F, Q, 768)
            return 0

        lax.fori_loop(0, 4, body, 0)

    def partial(c, send):
        def body(i, _):
            w = jnp.concatenate([W[g, u, i].reshape(768, T) for g, u in sts[2:]], axis=1)
            d = jnp.concatenate([DD[g, u, c].reshape(F * Q, T) for g, u in sts[2:]], axis=1)
            cs = pl.ds(pl.multiple_of(i * 768, 768), 768)
            r = Y[c, :, :, cs] + dot_nt(d, w).reshape(F, Q, 768)
            if send:
                SYS[:, :, cs] = r.astype(BF)
                sy_copy(i).start()
            else:
                Y[c, :, :, cs] = r
            return 0

        lax.fori_loop(0, 4, body, 0)

    def rs_copy(st, v, d, n):
        g, u = st
        step = 1 if d == 0 else -1
        axis = axis_of(v, 1)
        p = m4(pos_of(axis) + step * (2 if n == 0 else 1))
        h = d if n != 1 else 1 - d
        i = g * 4 + u * 2 + v
        return remote(heavy(GS.at[g, u], v, p, h), HR.at[g, u, v, d, n],
                      rs_s.at[i, d, n], rs_r.at[i, d, n], ring(axis, step))

    def rs_arrived(st, v, d, n):
        g, u = st
        i = g * 4 + u * 2 + v
        arrived(HR.at[g, u, v, d, n], rs_s.at[i, d, n], rs_r.at[i, d, n])

    def rs_start(st):
        for n in (0, 1):
            for v in (0, 1):
                for d in (0, 1):
                    rs_copy(st, v, d, n).start()

    def rs_fwd(st):
        g, u = st
        for v in (0, 1):
            axis = axis_of(v, 1)
            for d in (0, 1):
                rs_arrived(st, v, d, 0)
                ref = heavy(GS.at[g, u], v, m4(pos_of(axis) + (1 if d == 0 else -1)), d)
                ref[...] = (ref[...].astype(F32) + HR[g, u, v, d, 0].astype(F32)).astype(BF)
                rs_copy(st, v, d, 2).start()

    def rl_copy(st, v, i):
        g, u = st
        axis = axis_of(v, 0)
        j = g * 4 + u * 2 + v
        return remote(R1.at[g, u, v, m4(pos_of(axis) + i)], LR.at[g, u, v, i - 1],
                      rl_s.at[j, i], rl_r.at[j, i], ring(axis, i))

    def rs_turn(st):
        g, u = st
        for v in (0, 1):
            axis = axis_of(v, 1)
            for n in (1, 2):
                for d in (0, 1):
                    rs_arrived(st, v, d, n)
            for h in (0, 1):
                own = heavy(GS.at[g, u], v, pos_of(axis), h)[...].astype(F32)
                first = HR[g, u, v, 0, 2 if h == 0 else 1].astype(F32)
                second = HR[g, u, v, 1, 1 if h == 0 else 2].astype(F32)
                R1[g, u, v, 2 * h:2 * h + 2] = (own + first + second).astype(BF)
            for i in (1, 3, 2):
                rl_copy(st, v, i).start()

    def zr_copy(st, k):
        g, u = st
        return remote(R2.at[g, u, k], ZR.at[u, quarter], zr_s.at[g, u, k],
                      zr_r.at[u, quarter], at(k, group_of(core, me, g)))

    def rs_last(st):
        g, u = st
        for v in (0, 1):
            for i in (1, 3, 2):
                rl_copy(st, v, i).wait_recv()
            own = R1[g, u, v, pos_of(axis_of(v, 0))].astype(F32)
            R2[g, u, v] = (own + LR[g, u, v, 0].astype(F32) + LR[g, u, v, 1].astype(F32)
                           + LR[g, u, v, 2].astype(F32)).astype(BF)
            zr_copy(st, v).start()

    def all_attend(st):
        for c in (0, 1):
            for b in (0, 1):
                attend(st, c, b)

    proj(sts[0])
    ag_fwd(sts[2])
    lax.fori_loop(0, 8, turn, 0)
    da_wait(0)
    all_attend(sts[0])
    grads(sts[0])
    ag_fwd(sts[3])
    rs_start(sts[0])
    at_begin(sts[0])

    ag_done(sts[1])
    proj(sts[1])
    da_wait(1)
    all_attend(sts[1])
    grads(sts[1])
    rs_start(sts[1])
    at_begin(sts[1])
    partial_first()
    rs_fwd(sts[0])

    ag_done(sts[2])
    proj(sts[2])
    all_attend(sts[2])
    grads(sts[2])
    rs_start(sts[2])
    at_begin(sts[2])
    rs_fwd(sts[1])

    ag_done(sts[3])
    proj(sts[3])
    all_attend(sts[3])
    at_begin(sts[3])

    partial(1 - core, True)
    rs_turn(sts[0])
    rs_fwd(sts[2])
    partial(core, False)
    for i in range(4):
        sy_copy(i).wait_recv()

    def own_sum(n):
        f = frame(n)
        return Y[core, f] + SYR[f].astype(F32)

    def pp_copy(i):
        return remote(PS.at[i], PR.at[i], pp_s.at[i], pp_r.at[i], partner)

    def td_copy(i):
        return remote(TD.at[i], dtok_ref.at[rows_of(me)], td_s.at[i], td_r.at[i], at(core, frame(i)))

    for i in (1, 2, 3, 0):
        PS[i] = own_sum(4 + i).astype(BF)
        pp_copy(i).start()
    grads(sts[3])
    rs_start(sts[3])
    rs_turn(sts[1])
    rs_last(sts[0])

    def deliver(i):
        part = own_sum(i)
        pp_copy(i).wait_recv()
        tot = (part + PR[i].astype(F32)).astype(BF)
        if i:
            TD[i] = tot
            td_copy(i).start()
        else:
            dtok_ref[rows_of(me), :] = tot

    deliver(1)
    rs_fwd(sts[3])
    deliver(2)
    rs_turn(sts[2])
    rs_last(sts[1])
    deliver(3)
    rs_turn(sts[3])
    rs_last(sts[2])
    rs_last(sts[3])
    deliver(0)

    for st in sts:
        at_wait(st)
    for i in (1, 2, 3):
        arrived(dtok_ref.at[rows_of(tx_target(i))], td_s.at[i], td_r.at[i])
    for u in (0, 1):
        for q in range(4):
            arrived(ZR.at[u, q], zr_s.at[0, 0, 0], zr_r.at[u, q])
        tot = (ZR[u, 0].astype(F32) + ZR[u, 1].astype(F32)
               + ZR[u, 2].astype(F32) + ZR[u, 3].astype(F32))
        for t, ref in enumerate((gq_ref, gk_ref, gv_ref)):
            ref[:, u * 128:(u + 1) * 128] = tot[:, t * 128:(t + 1) * 128]

    for st in sts:
        for v in (0, 1):
            for d in (0, 1):
                for n in range(3):
                    ag_copy(st, v, d, n).wait_send()
                    rs_copy(st, v, d, n).wait_send()
            for i in (1, 2, 3):
                lt_copy(st, v, i).wait_send()
                rl_copy(st, v, i).wait_send()
            zr_copy(st, v).wait_send()
        for dc in (0, 1):
            for df in range(8):
                if dc or df:
                    at_copy(st, dc, df).wait_send()
    for g in (0, 1):
        for dc in (0, 1):
            for df in range(8):
                if dc or df:
                    da_copy(g, dc, df).wait_send()
    for t in range(4):
        for u in (0, 1):
            zw_copy(t, u).wait_send()
    for i in range(4):
        tp_copy(i).wait_send()
        pp_copy(i).wait_send()
        sy_copy(i).wait_send()
        if i:
            tx_copy(i).wait_send()
            td_copy(i).wait_send()
    cb_copy.wait_send()
    for n in range(8):
        ts_copy(n).wait_send()


def place(*refs):
    sem = refs[10]
    copies = [pltpu.make_async_copy(refs[i], refs[5 + i], sem.at[i]) for i in range(5)]
    for c in copies:
        c.start()
    for c in copies:
        c.wait()


def place(*refs):
    src, dst, buf = refs[0:5], refs[5:10], refs[10:15]
    get, put = refs[15:17]
    first = [pltpu.make_async_copy(src[i], buf[i], get.at[i]) for i in range(5)]
    second = [pltpu.make_async_copy(buf[i], dst[i], put.at[i]) for i in range(5)]
    for c in first:
        c.start()
    for a, b in zip(first, second):
        a.wait()
        b.start()
    for c in second:
        c.wait()


def tables():
    half = HEAD_DIM // 2
    inv = 10000.0 ** (-(2.0 * np.arange(half, dtype=np.float32)) / HEAD_DIM)
    angle = np.arange(F, dtype=np.float32)[:, None] * inv[None, :].astype(np.float32)
    c, s = np.cos(angle), np.sin(angle)
    return (np.concatenate([c, c], 1).astype(np.float32),
            np.concatenate([-s, s], 1).astype(np.float32))


def on_device(tokens, d_attn, frame_counts, w_query, w_key, w_value):
    cosine, sine = tables()
    any_ = pl.BlockSpec(memory_space=pl.ANY)
    vmem = pl.BlockSpec(memory_space=pltpu.VMEM)
    smem = pl.BlockSpec(memory_space=pltpu.SMEM)
    dma = pltpu.SemaphoreType.DMA
    outs = pl.pallas_call(
        kernel,
        out_shape=(
            jax.ShapeDtypeStruct((S, F * C), BF),
            jax.ShapeDtypeStruct((S, D), BF),
            jax.ShapeDtypeStruct((96, C), F32),
            jax.ShapeDtypeStruct((96, C), F32),
            jax.ShapeDtypeStruct((96, C), F32),
        ),
        in_specs=[smem, any_, any_, any_, any_, any_, vmem, vmem],
        out_specs=(vmem,) * 5,
        scratch_shapes=[
            pltpu.VMEM((2, F, Q, D), BF),
            pltpu.VMEM((D, 2 * F * Q), BF),
            pltpu.VMEM((2, 96, T), BF),
            pltpu.VMEM((2, 2, 4, 4, 2, 96, T), BF),
            pltpu.VMEM((2, 2, F, Q, C), BF),
            pltpu.VMEM((3, 2, F, Q, 128), BF),
            pltpu.VMEM((2, 2, 2, F, Q, T), BF),
            pltpu.VMEM((2, 2, F, Q, C), BF),
            pltpu.VMEM((2, F, Q, D), F32),
            pltpu.VMEM((2, 2, 4, 4, 2, 96, T), BF),
            pltpu.VMEM((2, 2, 2, 2, 3, 2, 96, T), BF),
            pltpu.VMEM((2, 2, 2, 4, 96, T), BF),
            pltpu.VMEM((2, 2, 2, 3, 96, T), BF),
            pltpu.VMEM((2, 2, 2, 96, T), BF),
            pltpu.VMEM((2, 4, 96, T), BF),
            pltpu.VMEM((F, Q, D), BF),
            pltpu.VMEM((F, Q, D), BF),
            pltpu.VMEM((4, Q, D), BF),
            pltpu.VMEM((4, Q, D), BF),
            pltpu.VMEM((4, Q, D), BF),
            pltpu.VMEM((2, 8, 128), jnp.int32),
            dma((13,)),
            dma((4, 2)), dma((2, 2, 2)),
            dma((8, 2, 3)), dma((8, 2, 3)),
            dma((4,)), dma((4,)),
            dma((4,)), dma((4,)),
            dma((8,)), dma((8,)),
            dma((2, 2, 8)), dma((2, 2, 8)),
            dma((4, 2, 8)), dma((4, 2, 8)),
            dma((8, 2, 3)), dma((8, 2, 3)),
            dma((2, 2, 2)), dma((2, 4)),
            dma((8,)), dma((8,)),
            dma((4,)), dma((4,)),
            dma((4,)), dma((4,)),
            dma((1,)), dma((1,)),
            dma((8, 4)), dma((8, 4)),
            dma((8, 4)), dma((8, 4)),
        ],
        compiler_params=pltpu.CompilerParams(
            collective_id=0, has_side_effects=True, vmem_limit_bytes=62 * 1024 * 1024),
        name="temporal_attention",
    )(
        frame_counts, tokens.reshape(S, D),
        d_attn.reshape(S, F * C), w_query, w_key, w_value, jnp.asarray(cosine), jnp.asarray(sine),
    )
    shapes = tuple(jax.ShapeDtypeStruct(o.shape, o.dtype) for o in outs)
    outs = pl.pallas_call(
        place,
        out_shape=shapes,
        in_specs=[any_] * 5,
        out_specs=(any_,) * 5,
        scratch_shapes=[pltpu.VMEM(o.shape, o.dtype) for o in outs] + [dma((5,)), dma((5,))],
        compiler_params=pltpu.CompilerParams(vmem_limit_bytes=62 * 1024 * 1024),
        name="place",
    )(*outs)
    attn, dtok, gq, gk, gv = outs
    return attn.reshape(d_attn.shape), dtok.reshape(tokens.shape), gq, gk, gv


def solution(mesh):
    return jax.shard_map(
        on_device,
        mesh=mesh,
        in_specs=(
            P("dp", "seq", None, None),
            P("dp", "seq", None, None),
            P("dp"),
            P("dp", "seq"),
            P("dp", "seq"),
            P("dp", "seq"),
        ),
        out_specs=(
            P("dp", "seq", None, None),
            P("dp", "seq", None, None),
            P("dp", "seq"),
            P("dp", "seq"),
            P("dp", "seq"),
        ),
        check_vma=False,
    )
```
